128 devices in a mesh: comp: 32 (over y, z, core), grp: 4 (over x).
Axes of the slice: x: 4, y: 4, z: 4, core: 2. Of those that a mesh axis runs over, the one named last changes fastest.
Arguments:
- spectrum: float32 [32, 36, 4, 64, 512], P('comp', None, 'grp'), may hold values from 0.05 to 1
- courant: float32 [32], P('comp'), may hold values from 0.15 to 0.45
- sea_mask: int32 [4, 64, 512], P('grp'), may hold values 0 or 1
- wind_u: float32 [4, 64, 512], P('grp', 'comp'), may hold values from -4 to 4
- wind_v: float32 [4, 64, 512], P('grp', 'comp'), may hold values from -4 to 4
- boundary_cells: int32 [40, 128], replicated, may hold values from 0 to 131071, as said below
Outputs:
- updated: float32 [32, 36, 4, 64, 512], P(None, None, 'grp', 'comp')
- boundary: float32 [32, 36, 40, 128], P('comp', None, 'grp')
The draws below stay inside these ranges and needn't reach their ends.
Inputs may be any that keep to these rules, and one draw needn't show every extreme that they name: `boundary_cells`: positions k * 32 to (k + 1) * 32 - 1 of every list name cells of row block k.
All inputs are finite; a program needn't handle non-finite values. No bound on the sum of `sea_mask` on one device may be relied on, other than what follows from the above.
Results may differ from the reference program's by a relative error of at most 0.000075.
Values sent between devices are 32-bit elements; how exact they have to be, the bound alone decides.
No kernel may reach another device: no remote copies, remote signals or barrier semaphores. Data moves between devices by JAX's collectives and lax.ppermute only.
A program may use at most 192 MiB of HBM per device.

```python
import math
import jax
import jax.numpy as jnp
from jax import lax

NDIR = 36
NFREQ = 32
SUBSTEPS = 3
NX = 512
ROWS_DEV = 64
BP_BLK = 32
BLOCKS = 4
NY = 256
NEST = 40
BP = 128


def draw_boundary_cells(key, part):
    key = jax.random.fold_in(key, 5)
    block_cells = ROWS_DEV * NX
    offsets = jax.random.randint(key, (NEST, BP), 0, block_cells)
    starts = jnp.arange(BP, dtype=jnp.int32) // BP_BLK * block_cells
    cells = offsets.astype(jnp.int32) + starts[None, :]
    cells = cells.at[0, 0].set(0)
    cells = cells.at[0, BP - 1].set(NY * NX - 1)
    return cells.astype(jnp.int32)


def set_ends(entries, key, low, high):
    longest = entries.shape.index(max(entries.shape))
    spots = []
    for shift in (0, 1):
        where = [jax.random.randint(jax.random.fold_in(key, axis), (), 0, length) for axis, length in enumerate(entries.shape)]
        where[longest] = (where[longest] + shift) % entries.shape[longest]
        spots.append(tuple(where))
    return entries.at[spots[0]].set(low).at[spots[1]].set(high)


def shard_levels(rng, dims, shards, least, largest):
    factor_of, own = 1.0, jax.random.fold_in(rng, 6)
    for axis_at, blocks in shards:
        draws = jnp.exp(jax.random.uniform(jax.random.fold_in(own, axis_at), (blocks,), jnp.float32, least / len(shards), largest / len(shards)))
        factor_of = factor_of * jnp.repeat(draws, dims[axis_at] // blocks).reshape([-1 if axis == axis_at else 1 for axis in range(len(dims))])
    return factor_of


def bell_draw(own_key, shape, scale, limit, shards=(), kind=jnp.bfloat16):
    factor_of = shard_levels(own_key, shape, shards, -0.22, 0.18) if shards else 1.0
    drawn = jax.random.normal(own_key, shape, jnp.float32) * scale * factor_of
    return jnp.minimum(jnp.maximum(drawn, -limit), limit).astype(kind)


def setup_inputs(seed: int = 0) -> dict:
    key_list = jax.random.split(jax.random.key(seed), 7)
    return {
        "spectrum": jnp.clip(jnp.exp(math.log(1.0) - 2.9957323 * jax.random.uniform(key_list[0], (NFREQ, NDIR, BLOCKS, ROWS_DEV, NX), jnp.float32) ** shard_levels(key_list[0], (NFREQ, NDIR, BLOCKS, ROWS_DEV, NX), ((0, 32), (2, 4)), -0.2, 0.2)), 0.05, 1.0),
        "courant": jnp.clip(jnp.exp(math.log(0.45) - 1.0986122 * jax.random.uniform(key_list[1], (NFREQ,), jnp.float32) ** shard_levels(key_list[1], (NFREQ,), ((0, 32),), -0.2, 0.2)), 0.15, 0.45),
        "sea_mask": set_ends((jax.random.randint(key_list[2], (BLOCKS, ROWS_DEV, NX), 0, 8) < 7).astype(jnp.int32), jax.random.fold_in(key_list[2], 1), 0, 1),
        "wind_u": bell_draw(key_list[3], (BLOCKS, ROWS_DEV, NX), 1.0, 4.0, ((0, 4), (1, 32)), jnp.float32),
        "wind_v": bell_draw(key_list[4], (BLOCKS, ROWS_DEV, NX), 1.0, 4.0, ((0, 4), (1, 32)), jnp.float32),
        "boundary_cells": draw_boundary_cells(jax.random.fold_in(key_list[6], 71), 0),
    }


def substep(extended, speed_east, speed_north, mask_float):
    energy = extended[:, 1:-1]
    south = extended[:, :-2]
    north = extended[:, 2:]
    west = jnp.roll(energy, 1, axis=2)
    east = jnp.roll(energy, -1, axis=2)
    flux = jnp.maximum(speed_east, 0.0) * (energy - west) + jnp.maximum(-speed_east, 0.0) * (energy - east)
    flux = flux + jnp.maximum(speed_north, 0.0) * (energy - south) + jnp.maximum(-speed_north, 0.0) * (energy - north)
    return mask_float * (energy - flux)


def sources(energy, wind_east, wind_north):
    extra = (1,) * (energy.ndim - 2)
    scale = 0.3 * 1.1 ** jnp.arange(NFREQ, dtype=jnp.float32)
    wavenum = scale * scale
    theta = 2.0 * jnp.pi * jnp.arange(NDIR, dtype=jnp.float32) / NDIR
    scale_b = scale.reshape((NFREQ, 1) + extra)
    wave_b = wavenum.reshape((NFREQ, 1) + extra)
    cos_b = jnp.cos(theta).reshape((1, NDIR) + extra)
    sin_b = jnp.sin(theta).reshape((1, NDIR) + extra)
    mean_energy = jnp.mean(energy, axis=(0, 1))
    mean_wave = jnp.mean(energy * wave_b, axis=(0, 1))
    ratio = jnp.maximum(mean_energy, 0.05) / jnp.maximum(mean_wave, 0.1)
    projected = wind_east * cos_b + wind_north * sin_b
    gain = 0.05 * scale_b * jnp.maximum(projected * scale_b - 1.0, 0.0)
    steep = mean_energy / 0.3
    loss = 0.1 * scale_b * wave_b * ratio * (steep * steep)
    return energy * jnp.exp(gain - loss)


def reference(spectrum, courant, sea_mask, wind_u, wind_v, boundary_cells):
    theta = 2.0 * jnp.pi * jnp.arange(NDIR, dtype=jnp.float32) / NDIR
    speed_east = courant[:, None] * jnp.cos(theta)[None, :]
    speed_north = courant[:, None] * jnp.sin(theta)[None, :]
    energy = spectrum.reshape(NFREQ, NDIR, NY, NX)
    mask_float = sea_mask.astype(jnp.float32).reshape(1, NY, NX)

    def advance(packed_items):
        spectra_block, east_speed, north_speed = packed_items
        for turn_index in range(SUBSTEPS):
            extended = jnp.pad(spectra_block, ((0, 0), (1, 1), (0, 0)))
            spectra_block = substep(extended, east_speed[:, None, None], north_speed[:, None, None], mask_float)
        return spectra_block

    propagated = lax.map(advance, (energy, speed_east, speed_north))
    boundary = propagated.reshape(NFREQ, NDIR, NY * NX)[:, :, boundary_cells]
    updated = sources(propagated.reshape(NFREQ, NDIR, BLOCKS, ROWS_DEV, NX), wind_u, wind_v)
    return updated, boundary
```

```python
import functools

import jax
import jax.numpy as jnp
import numpy as np
from jax import lax
from jax.experimental import pallas as pl
from jax.experimental.pallas import tpu as pltpu
from jax.sharding import PartitionSpec as P

NDIR = 36
NFREQ = 32
SUBSTEPS = 3
HALF = NDIR // 2
QUART = NDIR // 4
ROWS = 64
COLS = 512
LANES = 128
TILES = COLS // LANES
HALO = 3
SLOT = HALO * TILES
PACK = 240
MARGIN = 24
VMEM_LIMIT = 56 * 1024 * 1024

THETA = (2.0 * np.pi * np.arange(NDIR) / NDIR).astype(np.float32)
COS = np.cos(THETA).astype(np.float32)
SIN = np.sin(THETA).astype(np.float32)
SCALE = (0.3 * np.float32(1.1) ** np.arange(NFREQ, dtype=np.float32)).astype(np.float32)
LOG2E = 1.4426950408889634


def pack_kernel(last_ref, first_ref, mask_ref, up_ref, down_ref):
    for out, src, low, row in ((up_ref, last_ref, 5, 56), (down_ref, first_ref, 0, 0)):
        for d in range(HALF):
            for j in range(TILES):
                out[pl.ds(d * SLOT + j, HALO, stride=TILES), :] = src[
                    d, low : low + HALO, j * LANES : (j + 1) * LANES
                ]
        m = mask_ref[0, row : row + 8, :].astype(jnp.float32)
        for j in range(TILES):
            out[pl.ds(HALF * SLOT + j, HALO, stride=TILES), :] = m[
                low : low + HALO, j * LANES : (j + 1) * LANES
            ]
        out[(HALF + 1) * SLOT :, :] = jnp.zeros((PACK - (HALF + 1) * SLOT, LANES), jnp.float32)


def pack(spectrum, sea_mask):
    block = (HALF, 8, COLS)
    out = jax.ShapeDtypeStruct((PACK, LANES), jnp.float32)
    return pl.pallas_call(
        pack_kernel,
        grid=(1,),
        in_specs=[
            pl.BlockSpec(block, lambda i: (0, ROWS // 8 - 1, 0)),
            pl.BlockSpec(block, lambda i: (1, 0, 0)),
            pl.BlockSpec((1, ROWS, COLS), lambda i: (0, 0, 0)),
        ],
        out_specs=[pl.BlockSpec((PACK, LANES), lambda i: (0, 0))] * 2,
        out_shape=[out, out],
        compiler_params=pltpu.CompilerParams(vmem_limit_bytes=VMEM_LIMIT),
        name="pack",
    )(spectrum, spectrum, sea_mask)


def propagate_kernel(per, courant_ref, trig_ref, e_ref, mask_ref, south_ref, north_ref, out_ref, mask_s, mask_n, halo_s):
    step = pl.program_id(0)

    def halo_tile(slot, low):
        parts = [
            halo_s[pl.ds(MARGIN + slot * SLOT + j - low * TILES, 8, stride=TILES), :]
            for j in range(TILES)
        ]
        return jnp.concatenate(parts, axis=1)

    def load_halo(src):
        halo_s[0:MARGIN, :] = jnp.zeros((MARGIN, LANES), jnp.float32)
        halo_s[MARGIN : MARGIN + PACK, :] = src[...]

    @pl.when(step == 0)
    def _():
        load_halo(south_ref)
        m = mask_ref[0].astype(jnp.float32)
        mask_s[8:, :] = m
        mask_s[:8, :] = halo_tile(HALF, 5)
        mask_n[:ROWS, :] = m

    @pl.when(step == HALF // per)
    def _():
        load_halo(north_ref)
        mask_n[ROWS:, :] = halo_tile(HALF, 0)

    flat = out_ref.reshape(32 * per * 8, LANES)

    def advance(south, west):
        def body(k, carry):
            d = step * per + k
            slot = d if south else d - HALF
            a = courant_ref[0] * trig_ref[0, d]
            b = courant_ref[0] * trig_ref[1, d]
            c = 1.0 - a - b
            e = e_ref[k]
            if south:
                e = jnp.concatenate([halo_tile(slot, 5), e], axis=0)
                m = mask_s[...]
            else:
                e = jnp.concatenate([e, halo_tile(slot, 0)], axis=0)
                m = mask_n[...]
            for _ in range(SUBSTEPS):
                x = pltpu.roll(e, 1 if west else COLS - 1, 1)
                y = pltpu.roll(e, 1 if south else ROWS + 7, 0)
                e = m * (c * e + a * x + b * y)
            e = e[8:] if south else e[:ROWS]
            for j in range(TILES):
                flat[pl.ds(j, ROWS, stride=TILES), :] = e[:, j * LANES : (j + 1) * LANES]
            return carry

        lax.fori_loop(0, per, body, 0)

    quarter = step // (QUART // per)
    for q, (south, west) in enumerate(((True, True), (True, False), (False, False), (False, True))):
        pl.when(quarter == q)(functools.partial(advance, south, west))


def propagate(spectrum, courant, sea_mask, from_south, from_north):
    per = 1
    trig = jnp.asarray(np.stack([np.abs(COS), np.abs(SIN)]))
    whole = lambda *shape: pl.BlockSpec(shape, lambda i: (0,) * len(shape))
    return pl.pallas_call(
        functools.partial(propagate_kernel, per),
        grid=(NDIR // per,),
        in_specs=[
            pl.BlockSpec(memory_space=pltpu.SMEM),
            pl.BlockSpec(memory_space=pltpu.SMEM),
            pl.BlockSpec((per, ROWS, COLS), lambda i: (i, 0, 0)),
            whole(1, ROWS, COLS),
            whole(PACK, LANES),
            whole(PACK, LANES),
        ],
        out_specs=pl.BlockSpec((32, per, 8, LANES), lambda i: (0, i, 0, 0)),
        out_shape=jax.ShapeDtypeStruct((32, NDIR, 8, LANES), jnp.float32),
        scratch_shapes=[
            pltpu.VMEM((ROWS + 8, COLS), jnp.float32),
            pltpu.VMEM((ROWS + 8, COLS), jnp.float32),
            pltpu.VMEM((MARGIN + PACK + 16, LANES), jnp.float32),
        ],
        compiler_params=pltpu.CompilerParams(vmem_limit_bytes=VMEM_LIMIT),
        name="propagate",
    )(courant, trig, spectrum, sea_mask, from_south, from_north)


def pick_kernel(grp_ref, cells_ref, p_ref, *out_refs):
    group = grp_ref[0]
    count = len(out_refs)
    lane = lax.broadcasted_iota(jnp.int32, (NDIR, LANES), 1)
    points = LANES // count
    for k, out in enumerate(out_refs):
        owner = lax.rem(group + k, count)
        nests = out.shape[0]

        def nest_body(n, carry):
            def point_body(p, acc):
                for u in range(8):
                    col = group * points + p * 8 + u
                    cell = cells_ref[owner * nests + n, col] - group * (ROWS * COLS)
                    y = lax.shift_right_logical(cell, 9)
                    x = lax.bitwise_and(cell, COLS - 1)
                    row = lax.shift_right_logical(y, 1) * (NDIR * 8) + lax.bitwise_and(y, 1) * 4 + lax.shift_right_logical(x, 7)
                    got = p_ref[pl.ds(row, NDIR, stride=8), :]
                    turn = lax.bitwise_and(col - x, LANES - 1)
                    acc = jnp.where(lane == col, pltpu.roll(got, turn, 1), acc)
                return acc

            out[n] = lax.fori_loop(0, points // 8, point_body, jnp.zeros((NDIR, LANES), jnp.float32))
            return carry

        lax.fori_loop(0, nests, nest_body, 0)


def pick(group, cells, moved, count):
    nests = cells.shape[0] // count
    return pl.pallas_call(
        pick_kernel,
        in_specs=[
            pl.BlockSpec(memory_space=pltpu.SMEM),
            pl.BlockSpec(memory_space=pltpu.SMEM),
            pl.BlockSpec(memory_space=pltpu.VMEM),
        ],
        out_specs=[pl.BlockSpec(memory_space=pltpu.VMEM)] * count,
        out_shape=[jax.ShapeDtypeStruct((nests, NDIR, LANES), jnp.float32)] * count,
        compiler_params=pltpu.CompilerParams(vmem_limit_bytes=VMEM_LIMIT),
        cost_estimate=pl.CostEstimate(flops=10_000_000, bytes_accessed=6_000_000, transcendentals=0),
        name="pick",
    )(group, cells, moved.reshape(32 * NDIR * 8, LANES))


def merge_kernel(*refs):
    *ins, out = refs
    for n in range(ins[0].shape[0]):
        total = ins[0][n]
        for r in ins[1:]:
            total = total + r[n]
        out[:, n, :] = total


def merge(parts):
    nests = parts[0].shape[0]
    return pl.pallas_call(
        merge_kernel,
        out_shape=jax.ShapeDtypeStruct((NDIR, nests, LANES), jnp.float32),
        name="merge",
    )(*parts)


FCHUNK = 4
NCHUNK = NFREQ // FCHUNK


def source_kernel(recv_ref, u_ref, v_ref, out_ref, buf, outbuf, sem, osem):
    for c in range(NCHUNK):
        pltpu.make_async_copy(recv_ref.at[pl.ds(c * FCHUNK, FCHUNK)], buf.at[pl.ds(c * FCHUNK, FCHUNK)], sem.at[c]).start()
    total = jnp.zeros((8, LANES), jnp.float32)
    weighted = jnp.zeros((8, LANES), jnp.float32)
    for c in range(NCHUNK):
        pltpu.make_async_copy(recv_ref.at[pl.ds(c * FCHUNK, FCHUNK)], buf.at[pl.ds(c * FCHUNK, FCHUNK)], sem.at[c]).wait()
        for i in range(FCHUNK):
            f = c * FCHUNK + i
            s = jnp.sum(buf[f], axis=0)
            total = total + s
            weighted = weighted + s * float(SCALE[f] * SCALE[f])
    m0 = total * (1.0 / (NFREQ * NDIR))
    q = weighted * (1.0 / (NFREQ * NDIR))
    ratio = jnp.maximum(m0, 0.05) / jnp.maximum(q, 0.1)
    steep = m0 / 0.3
    base = ratio * (steep * steep)
    sub = lax.broadcasted_iota(jnp.int32, (8, LANES), 0)
    order = lax.rem(sub, 2) * 4 + lax.div(sub, 2)
    shuffle = lambda value: jnp.take_along_axis(value, order, axis=0)
    base = shuffle(base)
    u = u_ref[...]
    v = v_ref[...]

    for c in range(NCHUNK):
        fs = range(c * FCHUNK, (c + 1) * FCHUNK)
        loss = [base * float(0.1 * SCALE[f] ** 3 * LOG2E) for f in fs]
        for d in range(NDIR):
            proj = u * float(COS[d]) + v * float(SIN[d])
            for i, f in enumerate(fs):
                gain = jnp.maximum(proj * float(0.05 * SCALE[f] ** 2 * LOG2E) - float(0.05 * SCALE[f] * LOG2E), 0.0)
                outbuf[f, d] = shuffle(buf[f, d]) * jnp.exp2(gain - loss[i])
        pltpu.make_async_copy(outbuf.at[pl.ds(c * FCHUNK, FCHUNK)], out_ref.at[pl.ds(c * FCHUNK, FCHUNK)], osem.at[c]).start()
    for c in range(NCHUNK):
        pltpu.make_async_copy(outbuf.at[pl.ds(c * FCHUNK, FCHUNK)], out_ref.at[pl.ds(c * FCHUNK, FCHUNK)], osem.at[c]).wait()


def sources(recv, wind_u, wind_v):
    tile = lambda w: w.reshape(2, TILES, LANES).transpose(1, 0, 2).reshape(8, LANES)
    shape = (NFREQ, NDIR, 8, LANES)
    out = pl.pallas_call(
        source_kernel,
        in_specs=[
            pl.BlockSpec(memory_space=pl.ANY),
            pl.BlockSpec(memory_space=pltpu.VMEM),
            pl.BlockSpec(memory_space=pltpu.VMEM),
        ],
        out_specs=pl.BlockSpec(memory_space=pl.ANY),
        out_shape=jax.ShapeDtypeStruct(shape, jnp.float32),
        scratch_shapes=[
            pltpu.VMEM(shape, jnp.float32),
            pltpu.VMEM(shape, jnp.float32),
            pltpu.SemaphoreType.DMA((NCHUNK,)),
            pltpu.SemaphoreType.DMA((NCHUNK,)),
        ],
        compiler_params=pltpu.CompilerParams(vmem_limit_bytes=VMEM_LIMIT),
        name="sources",
    )(recv, tile(wind_u), tile(wind_v))
    out = out.reshape(NFREQ, NDIR, TILES, 2, LANES).transpose(0, 1, 3, 2, 4)
    return out.reshape(NFREQ, NDIR, 1, 2, COLS)


def per_device(spectrum, courant, sea_mask, wind_u, wind_v, boundary_cells):
    size = lax.axis_size("grp")
    group = lax.axis_index("grp").astype(jnp.int32).reshape(1)
    block = spectrum.reshape(NDIR, ROWS, COLS)
    up, down = pack(block, sea_mask)
    from_south = lax.ppermute(up, "grp", [(i, i + 1) for i in range(size - 1)])
    from_north = lax.ppermute(down, "grp", [(i + 1, i) for i in range(size - 1)])
    result = propagate(block, courant, sea_mask, from_south, from_north)
    moved = lax.all_to_all(result, "comp", split_axis=0, concat_axis=0, tiled=True)
    picked = pick(group, boundary_cells, result, size)
    parts = [picked[0]]
    for k in range(1, size):
        parts.append(lax.ppermute(picked[k], "grp", [(i, (i + k) % size) for i in range(size)]))
    boundary = merge(parts)[None]
    updated = sources(moved, wind_u.reshape(2, COLS), wind_v.reshape(2, COLS))
    return updated, boundary


def solution(mesh):
    placed = (
        P("comp", None, "grp", None, None),
        P("comp"),
        P("grp", None, None),
        P("grp", "comp", None),
        P("grp", "comp", None),
        P(),
    )
    return jax.shard_map(
        per_device,
        mesh=mesh,
        in_specs=placed,
        out_specs=(P(None, None, "grp", "comp", None), P("comp", None, "grp", None)),
        check_vma=False,
    )
```

```python
import functools

import jax
import jax.numpy as jnp
import numpy as np
from jax import lax
from jax.experimental import pallas as pl
from jax.experimental.pallas import tpu as pltpu
from jax.sharding import PartitionSpec as P

NDIR = 36
NFREQ = 32
SUBSTEPS = 3
HALF = NDIR // 2
QUART = NDIR // 4
ROWS = 64
COLS = 512
LANES = 128
TILES = COLS // LANES
HALO = 3
EDGE = 4
SLOT = HALO * HALF + 2
PACK = TILES * SLOT
ROWBLOCK = TILES * 8
VMEM_LIMIT = 56 * 1024 * 1024

THETA = (2.0 * np.pi * np.arange(NDIR) / NDIR).astype(np.float32)
COS = np.cos(THETA).astype(np.float32)
SIN = np.sin(THETA).astype(np.float32)
SCALE = (0.3 * np.float32(1.1) ** np.arange(NFREQ, dtype=np.float32)).astype(np.float32)
LOG2E = 1.4426950408889634


def tiled(value):
    lead = value.shape[:-2]
    n = len(lead)
    value = value.reshape(*lead, ROWS // 8, 8, TILES, LANES)
    return value.transpose(*range(n), n, n + 2, n + 1, n + 3)


def groups():
    return ((0, 8), (8, 8), (16, 2))


def pack_kernel(spectrum_ref, mask_ref, up_ref, down_ref, last, first, sem):
    copies = [
        pltpu.make_async_copy(spectrum_ref.at[pl.ds(0, HALF), ROWS // 8 - 1], last, sem.at[0]),
        pltpu.make_async_copy(spectrum_ref.at[pl.ds(HALF, HALF), 0], first, sem.at[1]),
    ]
    for c in copies:
        c.start()
    flat_mask = mask_ref.reshape(ROWS * TILES, LANES)
    for c, out, src, low, mrow in (
        (copies[0], up_ref, last, 5, (ROWS // 8 - 1) * ROWBLOCK + 6),
        (copies[1], down_ref, first, 0, 0),
    ):
        for j in range(TILES):
            m = flat_mask[mrow + j * 8 : mrow + j * 8 + 2, :]
            out[j * SLOT + HALO * HALF : (j + 1) * SLOT, :] = m.astype(jnp.float32)
        c.wait()
        flat = src.reshape(HALF * ROWBLOCK, LANES)
        for j in range(TILES):
            for h in range(HALO):
                for g, n in groups():
                    row = j * SLOT + h * HALF + g
                    out[row : row + n, :] = flat[pl.ds(g * ROWBLOCK + j * 8 + low + h, n, stride=ROWBLOCK), :]


def pack(spectrum, mask):
    out = jax.ShapeDtypeStruct((PACK, LANES), jnp.float32)
    edge = pltpu.VMEM((HALF, TILES, 8, LANES), jnp.float32)
    return pl.pallas_call(
        pack_kernel,
        in_specs=[pl.BlockSpec(memory_space=pl.ANY), pl.BlockSpec(memory_space=pltpu.VMEM)],
        out_specs=[pl.BlockSpec(memory_space=pltpu.VMEM)] * 2,
        out_shape=[out, out],
        scratch_shapes=[edge, edge, pltpu.SemaphoreType.DMA((2,))],
        compiler_params=pltpu.CompilerParams(vmem_limit_bytes=VMEM_LIMIT),
        name="pack",
    )(spectrum, mask)


def interior_kernel(per, courant_ref, trig_ref, e_ref, mask_ref, out_ref, mask_s):
    step = pl.program_id(0)
    lane = lax.broadcasted_iota(jnp.int32, (8, LANES), 1)
    flat = out_ref.reshape(32 * per * 8, LANES)
    src = e_ref.reshape(per * ROWS * TILES, LANES)

    @pl.when(step == 0)
    def _():
        flat_mask = mask_ref.reshape(ROWS * TILES, LANES)
        for t in range(8):
            for j in range(TILES):
                mask_s[t, j] = flat_mask[pl.ds(j * 8 + t, 8, stride=ROWBLOCK), :].astype(jnp.float32)

    def advance(south, west):
        def body(k, carry):
            d = step * per + k
            a = courant_ref[0] * trig_ref[0, d]
            b = courant_ref[0] * trig_ref[1, d]
            c = 1.0 - a - b
            e = [
                [src[pl.ds(k * ROWS * TILES + j * 8 + t, 8, stride=ROWBLOCK), :] for j in range(TILES)]
                for t in range(8)
            ]
            for _ in range(SUBSTEPS):
                if south:
                    wrap = [pltpu.roll(e[7][j], 1, 0) for j in range(TILES)]
                else:
                    wrap = [pltpu.roll(e[0][j], 7, 0) for j in range(TILES)]
                new = [None] * 8
                for t in range(8):
                    if south:
                        y = e[t - 1] if t > 0 else wrap
                    else:
                        y = e[t + 1] if t < 7 else wrap
                    r = [pltpu.roll(e[t][j], 1 if west else LANES - 1, 1) for j in range(TILES)]
                    row = []
                    for j in range(TILES):
                        if west:
                            x = jnp.where(lane == 0, r[j - 1], r[j])
                        else:
                            x = jnp.where(lane == LANES - 1, r[(j + 1) % TILES], r[j])
                        row.append(mask_s[t, j] * (c * e[t][j] + a * x + b * y[j]))
                    new[t] = row
                e = new
            for t in range(8):
                for j in range(TILES):
                    row = (t // 2) * per * 8 + k * 8 + 2 * j + t % 2
                    flat[pl.ds(row, 8, stride=ROWBLOCK * per), :] = e[t][j]
            return carry

        lax.fori_loop(0, per, body, 0)

    quarter = step // (QUART // per)
    for q, (south, west) in enumerate(((True, True), (True, False), (False, False), (False, True))):
        pl.when(quarter == q)(functools.partial(advance, south, west))


def interior(spectrum, courant, mask):
    per = PER
    trig = jnp.asarray(np.stack([np.abs(COS), np.abs(SIN)]))
    return pl.pallas_call(
        functools.partial(interior_kernel, per),
        grid=(NDIR // per,),
        in_specs=[
            pl.BlockSpec(memory_space=pltpu.SMEM),
            pl.BlockSpec(memory_space=pltpu.SMEM),
            pl.BlockSpec((per, ROWS // 8, TILES, 8, LANES), lambda i: (i, 0, 0, 0, 0)),
            pl.BlockSpec(memory_space=pltpu.VMEM),
        ],
        out_specs=pl.BlockSpec((32, per, 8, LANES), lambda i: (0, i, 0, 0)),
        out_shape=jax.ShapeDtypeStruct((32, NDIR, 8, LANES), jnp.float32),
        scratch_shapes=[pltpu.VMEM((8, TILES, 8, LANES), jnp.float32)],
        compiler_params=pltpu.CompilerParams(vmem_limit_bytes=VMEM_LIMIT),
        cost_estimate=pl.CostEstimate(flops=40_000_000, bytes_accessed=9_500_000, transcendentals=0),
        name="interior",
    )(courant, trig, spectrum, mask)


PER = 3


def edges_kernel(courant_ref, trig_ref, spectrum_ref, mask_ref, south_ref, north_ref, p_in, p_ref, first, last, out, sem):
    del p_in
    loads = [
        pltpu.make_async_copy(spectrum_ref.at[pl.ds(0, HALF), 0], first, sem.at[0]),
        pltpu.make_async_copy(spectrum_ref.at[pl.ds(HALF, HALF), ROWS // 8 - 1], last, sem.at[1]),
    ]
    for c in loads:
        c.start()
    lane = lax.broadcasted_iota(jnp.int32, (8, LANES), 1)
    sub = lax.broadcasted_iota(jnp.int32, (8, LANES), 0)
    flat_mask = mask_ref.reshape(ROWS * TILES, LANES)
    total = HALO + EDGE
    stores = []

    def eight(ref, start, n, stride):
        value = ref[pl.ds(start, n, stride=stride), :]
        if n < 8:
            value = jnp.concatenate([value, jnp.zeros((8 - n, LANES), jnp.float32)], axis=0)
        return value

    for side, (edge, halo) in enumerate(((first, south_ref), (last, north_ref))):
        south = side == 0
        loads[side].wait()
        flat = edge.reshape(HALF * ROWBLOCK, LANES)
        flat_out = out.at[side].reshape(2 * HALF * 8, LANES)
        own = lambda p: (p - HALO) if south else (7 - (p - HALO))
        base = 0 if south else (ROWS // 8 - 1) * ROWBLOCK
        m = []
        for p in range(total):
            row = []
            for j in range(TILES):
                if p < HALO:
                    at = j * SLOT + HALO * HALF + (p - 1 if south else HALO - 1 - p)
                    value = halo[at : at + 1, :] if p > 0 else None
                else:
                    at = base + j * 8 + own(p)
                    value = flat_mask[at : at + 1, :].astype(jnp.float32)
                row.append(value)
            m.append(row)
        for g, n in groups():
            a = courant_ref[0] * trig_ref[2 * side, g : g + 8, :]
            b = courant_ref[0] * trig_ref[2 * side + 1, g : g + 8, :]
            c = 1.0 - a - b
            turned = sub + g >= QUART
            e = []
            for p in range(total):
                row = []
                for j in range(TILES):
                    if p < HALO:
                        h = p if south else HALO - 1 - p
                        row.append(eight(halo, j * SLOT + h * HALF + g, n, 1))
                    else:
                        row.append(eight(flat, g * ROWBLOCK + j * 8 + own(p), n, ROWBLOCK))
                e.append(row)
            for k in range(SUBSTEPS):
                new = [None] * total
                for p in range(k + 1, total):
                    rw = [pltpu.roll(e[p][j], 1, 1) for j in range(TILES)]
                    re = [pltpu.roll(e[p][j], LANES - 1, 1) for j in range(TILES)]
                    row = []
                    for j in range(TILES):
                        xw = jnp.where(lane == 0, rw[j - 1], rw[j])
                        xe = jnp.where(lane == LANES - 1, re[(j + 1) % TILES], re[j])
                        x = jnp.where(turned, xe, xw) if south else jnp.where(turned, xw, xe)
                        row.append(m[p][j] * (c * e[p][j] + a * x + b * e[p - 1][j]))
                    new[p] = row
                e = new
            for p in range(HALO, total):
                y = p - HALO if south else EDGE - 1 - (p - HALO)
                for j in range(TILES):
                    at = ((y // 2) * HALF + g) * 8 + 2 * j + y % 2
                    flat_out[pl.ds(at, n, stride=8), :] = e[p][j][:n]
        target = p_ref.at[pl.ds(0 if south else 30, 2), pl.ds(0 if south else HALF, HALF)]
        copy = pltpu.make_async_copy(out.at[side], target, sem.at[2 + side])
        copy.start()
        stores.append(copy)
    for copy in stores:
        copy.wait()


def edges(spectrum, courant, mask, from_south, from_north, inner):
    table = np.zeros((4, 24, LANES), np.float32)
    for side in range(2):
        ds = slice(side * HALF, (side + 1) * HALF)
        table[2 * side, :HALF] = np.abs(COS[ds])[:, None]
        table[2 * side + 1, :HALF] = np.abs(SIN[ds])[:, None]
    edge = pltpu.VMEM((HALF, TILES, 8, LANES), jnp.float32)
    vmem = pl.BlockSpec(memory_space=pltpu.VMEM)
    hbm = pl.BlockSpec(memory_space=pl.ANY)
    return pl.pallas_call(
        edges_kernel,
        in_specs=[pl.BlockSpec(memory_space=pltpu.SMEM), vmem, hbm, vmem, vmem, vmem, hbm],
        out_specs=hbm,
        out_shape=jax.ShapeDtypeStruct(inner.shape, inner.dtype),
        scratch_shapes=[
            edge,
            edge,
            pltpu.VMEM((2, 2, HALF, 8, LANES), jnp.float32),
            pltpu.SemaphoreType.DMA((4,)),
        ],
        input_output_aliases={6: 0},
        compiler_params=pltpu.CompilerParams(vmem_limit_bytes=VMEM_LIMIT),
        name="edges",
    )(courant, jnp.asarray(table), spectrum, mask, from_south, from_north, inner)


def pick_kernel(grp_ref, cells_ref, p_ref, *out_refs):
    group = grp_ref[0]
    count = len(out_refs)
    lane = lax.broadcasted_iota(jnp.int32, (NDIR, LANES), 1)
    points = LANES // count
    for k, out in enumerate(out_refs):
        owner = lax.rem(group + k, count)
        nests = out.shape[0]

        def nest_body(n, carry):
            def point_body(p, acc):
                for u in range(8):
                    col = group * points + p * 8 + u
                    cell = cells_ref[owner * nests + n, col] - group * (ROWS * COLS)
                    y = lax.shift_right_logical(cell, 9)
                    x = lax.bitwise_and(cell, COLS - 1)
                    row = lax.shift_right_logical(y, 1) * (NDIR * 8) + lax.shift_right_logical(x, 7) * 2 + lax.bitwise_and(y, 1)
                    got = p_ref[pl.ds(row, NDIR, stride=8), :]
                    turn = lax.bitwise_and(col - x, LANES - 1)
                    acc = jnp.where(lane == col, pltpu.roll(got, turn, 1), acc)
                return acc

            out[n] = lax.fori_loop(0, points // 8, point_body, jnp.zeros((NDIR, LANES), jnp.float32))
            return carry

        lax.fori_loop(0, nests, nest_body, 0)


def pick(group, cells, moved, count):
    nests = cells.shape[0] // count
    return pl.pallas_call(
        pick_kernel,
        in_specs=[
            pl.BlockSpec(memory_space=pltpu.SMEM),
            pl.BlockSpec(memory_space=pltpu.SMEM),
            pl.BlockSpec(memory_space=pltpu.VMEM),
        ],
        out_specs=[pl.BlockSpec(memory_space=pltpu.VMEM)] * count,
        out_shape=[jax.ShapeDtypeStruct((nests, NDIR, LANES), jnp.float32)] * count,
        compiler_params=pltpu.CompilerParams(vmem_limit_bytes=VMEM_LIMIT),
        cost_estimate=pl.CostEstimate(flops=10_000_000, bytes_accessed=6_000_000, transcendentals=0),
        name="pick",
    )(group, cells, moved.reshape(32 * NDIR * 8, LANES))


def merge_kernel(*refs):
    *ins, out = refs
    for n in range(ins[0].shape[0]):
        total = ins[0][n]
        for r in ins[1:]:
            total = total + r[n]
        out[:, n, :] = total


def merge(parts):
    nests = parts[0].shape[0]
    return pl.pallas_call(
        merge_kernel,
        out_shape=jax.ShapeDtypeStruct((NDIR, nests, LANES), jnp.float32),
        name="merge",
    )(*parts)


FCHUNK = 4
NCHUNK = NFREQ // FCHUNK


def source_kernel(recv_ref, u_ref, v_ref, out_ref, buf, outbuf, sem, osem):
    for c in range(NCHUNK):
        pltpu.make_async_copy(recv_ref.at[pl.ds(c * FCHUNK, FCHUNK)], buf.at[pl.ds(c * FCHUNK, FCHUNK)], sem.at[c]).start()
    total = jnp.zeros((8, LANES), jnp.float32)
    weighted = jnp.zeros((8, LANES), jnp.float32)
    for c in range(NCHUNK):
        pltpu.make_async_copy(recv_ref.at[pl.ds(c * FCHUNK, FCHUNK)], buf.at[pl.ds(c * FCHUNK, FCHUNK)], sem.at[c]).wait()
        for i in range(FCHUNK):
            f = c * FCHUNK + i
            s = jnp.sum(buf[f], axis=0)
            total = total + s
            weighted = weighted + s * float(SCALE[f] * SCALE[f])
    m0 = total * (1.0 / (NFREQ * NDIR))
    q = weighted * (1.0 / (NFREQ * NDIR))
    ratio = jnp.maximum(m0, 0.05) / jnp.maximum(q, 0.1)
    steep = m0 / 0.3
    base = ratio * (steep * steep)
    u = u_ref[...]
    v = v_ref[...]

    for c in range(NCHUNK):
        fs = range(c * FCHUNK, (c + 1) * FCHUNK)
        loss = [base * float(0.1 * SCALE[f] ** 3 * LOG2E) for f in fs]
        for d in range(NDIR):
            proj = u * float(COS[d]) + v * float(SIN[d])
            for i, f in enumerate(fs):
                gain = jnp.maximum(proj * float(0.05 * SCALE[f] ** 2 * LOG2E) - float(0.05 * SCALE[f] * LOG2E), 0.0)
                outbuf[f, d] = buf[f, d] * jnp.exp2(gain - loss[i])
        pltpu.make_async_copy(outbuf.at[pl.ds(c * FCHUNK, FCHUNK)], out_ref.at[pl.ds(c * FCHUNK, FCHUNK)], osem.at[c]).start()
    for c in range(NCHUNK):
        pltpu.make_async_copy(outbuf.at[pl.ds(c * FCHUNK, FCHUNK)], out_ref.at[pl.ds(c * FCHUNK, FCHUNK)], osem.at[c]).wait()


def sources(recv, wind_u, wind_v):
    tile = lambda w: w.reshape(2, TILES, LANES).transpose(1, 0, 2).reshape(8, LANES)
    shape = (NFREQ, NDIR, 8, LANES)
    out = pl.pallas_call(
        source_kernel,
        in_specs=[
            pl.BlockSpec(memory_space=pl.ANY),
            pl.BlockSpec(memory_space=pltpu.VMEM),
            pl.BlockSpec(memory_space=pltpu.VMEM),
        ],
        out_specs=pl.BlockSpec(memory_space=pl.ANY),
        out_shape=jax.ShapeDtypeStruct(shape, jnp.float32),
        scratch_shapes=[
            pltpu.VMEM(shape, jnp.float32),
            pltpu.VMEM(shape, jnp.float32),
            pltpu.SemaphoreType.DMA((NCHUNK,)),
            pltpu.SemaphoreType.DMA((NCHUNK,)),
        ],
        compiler_params=pltpu.CompilerParams(vmem_limit_bytes=VMEM_LIMIT),
        name="sources",
    )(recv, tile(wind_u), tile(wind_v))
    out = out.reshape(NFREQ, NDIR, TILES, 2, LANES).transpose(0, 1, 3, 2, 4)
    return out.reshape(NFREQ, NDIR, 1, 2, COLS)


def per_device(spectrum, courant, sea_mask, wind_u, wind_v, boundary_cells):
    size = lax.axis_size("grp")
    group = lax.axis_index("grp").astype(jnp.int32).reshape(1)
    block = tiled(spectrum.reshape(NDIR, ROWS, COLS))
    mask = tiled(sea_mask.reshape(ROWS, COLS))
    up, down = pack(block, mask)
    from_south = lax.ppermute(up, "grp", [(i, i + 1) for i in range(size - 1)])
    from_north = lax.ppermute(down, "grp", [(i + 1, i) for i in range(size - 1)])
    inner = interior(block, courant, mask)
    result = edges(block, courant, mask, from_south, from_north, inner)
    moved = lax.all_to_all(result, "comp", split_axis=0, concat_axis=0, tiled=True)
    picked = pick(group, boundary_cells, result, size)
    parts = [picked[0]]
    for k in range(1, size):
        parts.append(lax.ppermute(picked[k], "grp", [(i, (i + k) % size) for i in range(size)]))
    boundary = merge(parts)[None]
    updated = sources(moved, wind_u.reshape(2, COLS), wind_v.reshape(2, COLS))
    return updated, boundary


def solution(mesh):
    placed = (
        P("comp", None, "grp", None, None),
        P("comp"),
        P("grp", None, None),
        P("grp", "comp", None),
        P("grp", "comp", None),
        P(),
    )
    return jax.shard_map(
        per_device,
        mesh=mesh,
        in_specs=placed,
        out_specs=(P(None, None, "grp", "comp", None), P("comp", None, "grp", None)),
        check_vma=False,
    )
```

```python
import functools

import jax
import jax.numpy as jnp
import numpy as np
from jax import lax
from jax.experimental import pallas as pl
from jax.experimental.pallas import tpu as pltpu
from jax.sharding import PartitionSpec as P

NDIR = 36
NFREQ = 32
SUBSTEPS = 3
HALF = NDIR // 2
QUART = NDIR // 4
ROWS = 64
COLS = 512
LANES = 128
TILES = COLS // LANES
HALO = 3
SLOTS = HALF + 2
SLOT = TILES * HALO
ROWBLOCK = TILES * 8
MIB = 1024 * 1024

THETA = (2.0 * np.pi * np.arange(NDIR) / NDIR).astype(np.float32)
COS = np.cos(THETA).astype(np.float32)
SIN = np.sin(THETA).astype(np.float32)
SCALE = (0.3 * np.float32(1.1) ** np.arange(NFREQ, dtype=np.float32)).astype(np.float32)
LOG2E = 1.4426950408889634


def tiled(value):
    lead = value.shape[:-2]
    n = len(lead)
    value = value.reshape(*lead, ROWS // 8, 8, TILES, LANES)
    return value.transpose(*range(n), n, n + 2, n + 1, n + 3)


def in_hbm(value):
    return pltpu.with_memory_space_constraint(value, pltpu.HBM)


def pack_kernel(spectrum_ref, mask_ref, up_ref, down_ref, mask_s, sem):
    sides = ((up_ref, 0, ROWS // 8 - 1, 8 - HALO), (down_ref, HALF, 0, 0))
    copies = []
    for side, (out, d, tile, low) in enumerate(sides):
        for k, (src, dst) in enumerate((
            (spectrum_ref.at[pl.ds(d, HALF), tile, :, pl.ds(low, HALO)], out.at[pl.ds(0, HALF)]),
            (mask_ref.at[tile, :, pl.ds(low, HALO)], mask_s.at[side]),
        )):
            copies.append(pltpu.make_async_copy(src, dst, sem.at[2 * side + k]))
    for c in copies:
        c.start()
    for side in range(2):
        copies[2 * side + 1].wait()
        sides[side][0][HALF] = mask_s[side].astype(jnp.float32)
    for side in range(2):
        copies[2 * side].wait()


def pack(spectrum, mask):
    out = jax.ShapeDtypeStruct((SLOTS, TILES, HALO, 1, LANES), jnp.float32)
    up, down = pl.pallas_call(
        pack_kernel,
        in_specs=[pl.BlockSpec(memory_space=pl.ANY)] * 2,
        out_specs=[pl.BlockSpec(memory_space=pltpu.VMEM)] * 2,
        out_shape=[out, out],
        scratch_shapes=[pltpu.VMEM((2, TILES, HALO, 1, LANES), jnp.int32), pltpu.SemaphoreType.DMA((4,))],
        compiler_params=pltpu.CompilerParams(vmem_limit_bytes=2 * MIB),
        name="pack",
    )(in_hbm(spectrum[..., None, :]), in_hbm(mask[..., None, :]))
    return up.reshape(SLOTS * SLOT, LANES), down.reshape(SLOTS * SLOT, LANES)


FETCH = 3
INTER = FETCH


def propagate_kernel(
    courant_ref, trig_ref, table_ref, e_ref, mask_ref, south_ref, north_ref, out_ref, e_buf, out_buf, mask_s, edge_s, sem, out_sem
):
    fetch = lambda c: pltpu.make_async_copy(e_ref.at[pl.ds(c * FETCH, FETCH)], e_buf.at[pl.ds(c * FETCH, FETCH)], sem.at[c])
    put = lambda c: pltpu.make_async_copy(out_buf.at[:, pl.ds(c * FETCH, FETCH)], out_ref.at[:, pl.ds(c * FETCH, FETCH)], out_sem.at[c])
    for c in range(NDIR // FETCH):
        fetch(c).start()
    lane = lax.broadcasted_iota(jnp.int32, (8, LANES), 1)
    sub = lax.broadcasted_iota(jnp.int32, (8, LANES), 0)

    def shifted(row, west):
        r = [pltpu.roll(v, 1 if west else LANES - 1, 1) for v in row]
        if west:
            return [jnp.where(lane == 0, r[j - 1], r[j]) for j in range(TILES)]
        return [jnp.where(lane == LANES - 1, r[(j + 1) % TILES], r[j]) for j in range(TILES)]

    mask_s[...] = mask_ref[...].astype(jnp.float32)

    for side, halo in enumerate((south_ref, north_ref)):
        south = side == 0
        near = lambda p: HALO - 1 - p if south else p
        m = [[halo[HALF * SLOT + j * HALO + near(p) : HALF * SLOT + j * HALO + near(p) + 1, :] for j in range(TILES)] for p in range(2)]
        for g, n in ((0, 8), (8, 8), (16, 2)):
            a = courant_ref[0] * table_ref[2 * side, g : g + 8, :]
            b = courant_ref[0] * table_ref[2 * side + 1, g : g + 8, :]
            c = 1.0 - a - b
            turned = sub + g >= QUART
            rows = []
            for p in range(HALO):
                row = []
                for j in range(TILES):
                    v = halo[pl.ds(g * SLOT + j * HALO + near(p), n, stride=SLOT), :]
                    row.append(v if n == 8 else jnp.concatenate([v, jnp.zeros((8 - n, LANES), jnp.float32)], axis=0))
                rows.append(row)
            for k in range(HALO):
                for j in range(TILES):
                    edge_s[side, k, j, g : g + 8, :] = rows[0][j]
                new = []
                for p in range(len(rows) - 1):
                    w, e = shifted(rows[p], True), shifted(rows[p], False)
                    x = [jnp.where(turned, e[j], w[j]) if south else jnp.where(turned, w[j], e[j]) for j in range(TILES)]
                    new.append([m[p][j] * (c * rows[p][j] + a * x[j] + b * rows[p + 1][j]) for j in range(TILES)])
                rows = new

    def advance(south, west, first, i, carry):
        ds = [first + i * INTER + u for u in range(INTER)]
        many = range(INTER)
        side = 0 if south else 1
        at, turn = (0, 1) if south else (7, 7)
        fetch(first // FETCH + i).wait()
        a = [courant_ref[0] * trig_ref[0, d] for d in ds]
        b = [courant_ref[0] * trig_ref[1, d] for d in ds]
        c = [1.0 - x - y for x, y in zip(a, b)]
        e = [[[e_buf[d, t, j] for j in range(TILES)] for t in range(8)] for d in ds]
        for stage in range(SUBSTEPS):
            new = [[None] * 8 for _ in many]
            moved = [[[pltpu.roll(v, turn, 0) for v in row] for row in e[u]] for u in many]
            for t in range(8):
                for u in many:
                    if t == at:
                        beyond = [edge_s[side, stage, j, pl.ds(ds[u] - side * HALF, 1), :] for j in range(TILES)]
                    else:
                        beyond = moved[u][t - 1 if south else t + 1]
                    x = shifted(e[u][t], west)
                    y = [jnp.where(sub == at, beyond[j], moved[u][t][j]) for j in range(TILES)]
                    new[u][t] = [mask_s[t, j] * (c[u] * e[u][t][j] + a[u] * x[j] + b[u] * y[j]) for j in range(TILES)]
            e = new
        odd, high = sub & 2 != 0, sub >= 4
        for u in many:
            for t in range(8):
                v = e[u][t]
                w = [
                    jnp.where(odd, pltpu.roll(v[1], 2, 0), v[0]),
                    jnp.where(odd, v[1], pltpu.roll(v[0], 6, 0)),
                    jnp.where(odd, pltpu.roll(v[3], 2, 0), v[2]),
                    jnp.where(odd, v[3], pltpu.roll(v[2], 6, 0)),
                ]
                out_buf[4 * t, ds[u]] = jnp.where(high, pltpu.roll(w[2], 4, 0), w[0])
                out_buf[4 * t + 1, ds[u]] = jnp.where(high, pltpu.roll(w[3], 4, 0), w[1])
                out_buf[4 * t + 2, ds[u]] = jnp.where(high, w[2], pltpu.roll(w[0], 4, 0))
                out_buf[4 * t + 3, ds[u]] = jnp.where(high, w[3], pltpu.roll(w[1], 4, 0))
        put(first // FETCH + i).start()
        return carry

    for q, (south, west) in enumerate(((True, True), (True, False), (False, False), (False, True))):
        lax.fori_loop(0, QUART // INTER, functools.partial(advance, south, west, q * QUART), 0)
    for c in range(NDIR // FETCH):
        put(c).wait()


def propagate(spectrum, courant, mask, from_south, from_north):
    trig = np.stack([np.abs(COS), np.abs(SIN)])
    table = np.zeros((4, 24, LANES), np.float32)
    for side in range(2):
        ds = slice(side * HALF, (side + 1) * HALF)
        table[2 * side, :HALF] = np.abs(COS[ds])[:, None]
        table[2 * side + 1, :HALF] = np.abs(SIN[ds])[:, None]
    smem = pl.BlockSpec(memory_space=pltpu.SMEM)
    vmem = pl.BlockSpec(memory_space=pltpu.VMEM)
    return pl.pallas_call(
        propagate_kernel,
        in_specs=[smem, smem, vmem, pl.BlockSpec(memory_space=pl.ANY), vmem, vmem, vmem],
        out_specs=pl.BlockSpec(memory_space=pl.ANY),
        out_shape=pltpu.HBM((32, NDIR, 8, LANES), jnp.float32),
        scratch_shapes=[
            pltpu.VMEM((NDIR, ROWS // 8, TILES, 8, LANES), jnp.float32),
            pltpu.VMEM((32, NDIR, 8, LANES), jnp.float32),
            pltpu.VMEM((8, TILES, 8, LANES), jnp.float32),
            pltpu.VMEM((2, HALO, TILES, 24, LANES), jnp.float32),
            pltpu.SemaphoreType.DMA((NDIR // FETCH,)),
            pltpu.SemaphoreType.DMA((NDIR // FETCH,)),
        ],
        compiler_params=pltpu.CompilerParams(vmem_limit_bytes=13 * MIB),
        cost_estimate=pl.CostEstimate(flops=40_000_000, bytes_accessed=9_500_000, transcendentals=0),
        name="propagate",
    )(courant, jnp.asarray(trig), jnp.asarray(table), in_hbm(spectrum), mask, from_south, from_north)


def pick_kernel(grp_ref, cells_ref, p_ref, *out_refs):
    group = grp_ref[0]
    count = len(out_refs)
    lane = lax.broadcasted_iota(jnp.int32, (NDIR, LANES), 1)
    points = LANES // count
    for k, out in enumerate(out_refs):
        owner = lax.rem(group + k, count)
        nests = out.shape[0]

        def nest_body(n, carry):
            def point_body(p, acc):
                for u in range(8):
                    col = group * points + p * 8 + u
                    cell = lax.bitwise_and(cells_ref[owner * nests + n, col], ROWS * COLS - 1)
                    y = lax.shift_right_logical(cell, 9)
                    x = lax.bitwise_and(cell, COLS - 1)
                    row = lax.shift_right_logical(y, 1) * (NDIR * 8) + lax.shift_right_logical(x, 7) * 2 + lax.bitwise_and(y, 1)
                    got = p_ref[pl.ds(row, NDIR, stride=8), :]
                    turn = lax.bitwise_and(col - x, LANES - 1)
                    acc = jnp.where(lane == col, pltpu.roll(got, turn, 1), acc)
                return acc

            out[n] = lax.fori_loop(0, points // 8, point_body, jnp.zeros((NDIR, LANES), jnp.float32))
            return carry

        lax.fori_loop(0, nests, nest_body, 0)


def pick(group, cells, moved, count):
    nests = cells.shape[0] // count
    return pl.pallas_call(
        pick_kernel,
        in_specs=[
            pl.BlockSpec(memory_space=pltpu.SMEM),
            pl.BlockSpec(memory_space=pltpu.SMEM),
            pl.BlockSpec(memory_space=pltpu.VMEM),
        ],
        out_specs=[pl.BlockSpec(memory_space=pltpu.VMEM)] * count,
        out_shape=[jax.ShapeDtypeStruct((nests, NDIR, LANES), jnp.float32)] * count,
        compiler_params=pltpu.CompilerParams(vmem_limit_bytes=8 * MIB),
        cost_estimate=pl.CostEstimate(flops=10_000_000, bytes_accessed=6_000_000, transcendentals=0),
        name="pick",
    )(group, cells, moved.reshape(32 * NDIR * 8, LANES))


def merge_kernel(*refs):
    *ins, out = refs
    for n in range(ins[0].shape[0]):
        total = ins[0][n]
        for r in ins[1:]:
            total = total + r[n]
        out[:, n, :] = total


def merge(parts):
    nests = parts[0].shape[0]
    return pl.pallas_call(
        merge_kernel,
        out_shape=jax.ShapeDtypeStruct((NDIR, nests, LANES), jnp.float32),
        compiler_params=pltpu.CompilerParams(vmem_limit_bytes=4 * MIB),
        name="merge",
    )(*parts)


FCHUNK = 4
NCHUNK = NFREQ // FCHUNK


def source_kernel(recv_ref, u_ref, v_ref, out_ref, buf, outbuf, sem, osem):
    put = lambda c: pltpu.make_async_copy(
        outbuf.at[pl.ds(c * FCHUNK, FCHUNK)], out_ref.at[pl.ds(c * FCHUNK, FCHUNK)], osem.at[c]
    )
    fetch = lambda c: pltpu.make_async_copy(recv_ref.at[pl.ds(c * FCHUNK, FCHUNK)], buf.at[pl.ds(c * FCHUNK, FCHUNK)], sem.at[c])
    for c in range(NCHUNK):
        fetch(c).start()
    total = jnp.zeros((8, LANES), jnp.float32)
    weighted = jnp.zeros((8, LANES), jnp.float32)
    for f in range(NFREQ):
        if f % FCHUNK == 0:
            fetch(f // FCHUNK).wait()
        s = jnp.sum(buf[f], axis=0)
        total = total + s
        weighted = weighted + s * float(SCALE[f] * SCALE[f])
    m0 = total * (1.0 / (NFREQ * NDIR))
    q = weighted * (1.0 / (NFREQ * NDIR))
    ratio = jnp.maximum(m0, 0.05) / jnp.maximum(q, 0.1)
    steep = m0 / 0.3
    base = ratio * (steep * steep)
    u = u_ref[...]
    v = v_ref[...]

    for c in range(NCHUNK):
        fs = range(c * FCHUNK, (c + 1) * FCHUNK)
        loss = [base * float(0.1 * SCALE[f] ** 3 * LOG2E) for f in fs]
        for d in range(NDIR):
            proj = u * float(COS[d]) + v * float(SIN[d])
            for i, f in enumerate(fs):
                gain = jnp.maximum(proj * float(0.05 * SCALE[f] ** 2 * LOG2E) - float(0.05 * SCALE[f] * LOG2E), 0.0)
                outbuf[f, d] = buf[f, d] * jnp.exp2(gain - loss[i])
        put(c).start()
    for c in range(NCHUNK):
        put(c).wait()


def sources(recv, wind_u, wind_v):
    tile = lambda w: w.reshape(2, TILES, LANES).transpose(1, 0, 2).reshape(8, LANES)
    shape = (NFREQ, NDIR, 8, LANES)
    out = pl.pallas_call(
        source_kernel,
        in_specs=[pl.BlockSpec(memory_space=pl.ANY)] + [pl.BlockSpec(memory_space=pltpu.VMEM)] * 2,
        out_specs=pl.BlockSpec(memory_space=pltpu.HBM),
        out_shape=jax.ShapeDtypeStruct(shape, jnp.float32),
        scratch_shapes=[
            pltpu.VMEM(shape, jnp.float32),
            pltpu.VMEM(shape, jnp.float32),
            pltpu.SemaphoreType.DMA((NCHUNK,)),
            pltpu.SemaphoreType.DMA((NCHUNK,)),
        ],
        compiler_params=pltpu.CompilerParams(vmem_limit_bytes=12 * MIB),
        name="sources",
    )(in_hbm(recv), tile(wind_u), tile(wind_v))
    out = out.reshape(NFREQ, NDIR, TILES, 2, LANES).transpose(0, 1, 3, 2, 4)
    return out.reshape(NFREQ, NDIR, 1, 2, COLS)


def per_device(spectrum, courant, sea_mask, wind_u, wind_v, boundary_cells):
    size = lax.axis_size("grp")
    group = lax.axis_index("grp").astype(jnp.int32).reshape(1)
    block = tiled(spectrum.reshape(NDIR, ROWS, COLS))
    mask = tiled(sea_mask.reshape(ROWS, COLS))
    up, down = pack(block, mask)
    from_south = lax.ppermute(up, "grp", [(i, i + 1) for i in range(size - 1)])
    from_north = lax.ppermute(down, "grp", [(i + 1, i) for i in range(size - 1)])
    result = propagate(block, courant, mask, from_south, from_north)
    moved = lax.all_to_all(result, "comp", split_axis=0, concat_axis=0, tiled=True)
    picked = pick(group, boundary_cells, result, size)
    parts = [picked[0]]
    for k in range(1, size):
        parts.append(lax.ppermute(picked[k], "grp", [(i, (i + k) % size) for i in range(size)]))
    boundary = merge(parts)[None]
    updated = sources(moved, wind_u.reshape(2, COLS), wind_v.reshape(2, COLS))
    return updated, boundary


def solution(mesh):
    placed = (
        P("comp", None, "grp", None, None),
        P("comp"),
        P("grp", None, None),
        P("grp", "comp", None),
        P("grp", "comp", None),
        P(),
    )
    return jax.shard_map(
        per_device,
        mesh=mesh,
        in_specs=placed,
        out_specs=(P(None, None, "grp", "comp", None), P("comp", None, "grp", None)),
        check_vma=False,
    )
```

```python
import functools

import jax
import jax.numpy as jnp
import numpy as np
from jax import lax
from jax.experimental import pallas as pl
from jax.experimental.pallas import tpu as pltpu
from jax.sharding import PartitionSpec as P

NDIR = 36
NFREQ = 32
SUBSTEPS = 3
HALF = NDIR // 2
QUART = NDIR // 4
ROWS = 64
COLS = 512
LANES = 128
TILES = COLS // LANES
HALO = 3
SLOTS = HALF + 2
SLOT = TILES * HALO
ROWBLOCK = TILES * 8
MIB = 1024 * 1024

THETA = (2.0 * np.pi * np.arange(NDIR) / NDIR).astype(np.float32)
COS = np.cos(THETA).astype(np.float32)
SIN = np.sin(THETA).astype(np.float32)
SCALE = (0.3 * np.float32(1.1) ** np.arange(NFREQ, dtype=np.float32)).astype(np.float32)
LOG2E = 1.4426950408889634

ORDER = (15, 27, 28, 26, 22, 18, 24, 3, 9, 25, 6, 13, 7, 31, 20, 12, 1, 17, 23, 2, 30, 14, 16, 10, 0, 21, 5, 4, 8, 11, 19, 29)
PLACE = tuple(int(p) for p in np.argsort(ORDER))


def tiled(value):
    lead = value.shape[:-2]
    n = len(lead)
    value = value.reshape(*lead, ROWS // 8, 8, TILES, LANES)
    return value.transpose(*range(n), n, n + 2, n + 1, n + 3)


def in_hbm(value):
    return pltpu.with_memory_space_constraint(value, pltpu.HBM)


def pack_kernel(spectrum_ref, mask_ref, up_ref, down_ref, mask_s, sem):
    sides = ((up_ref, 0, ROWS // 8 - 1, 8 - HALO), (down_ref, HALF, 0, 0))
    copies = []
    for side, (out, d, tile, low) in enumerate(sides):
        for k, (src, dst) in enumerate((
            (spectrum_ref.at[pl.ds(d, HALF), tile, :, pl.ds(low, HALO)], out.at[pl.ds(0, HALF)]),
            (mask_ref.at[tile, :, pl.ds(low, HALO)], mask_s.at[side]),
        )):
            copies.append(pltpu.make_async_copy(src, dst, sem.at[2 * side + k]))
    for c in copies:
        c.start()
    for side in range(2):
        copies[2 * side + 1].wait()
        sides[side][0][HALF] = mask_s[side].astype(jnp.float32)
    for side in range(2):
        copies[2 * side].wait()


def pack(spectrum, mask):
    out = jax.ShapeDtypeStruct((SLOTS, TILES, HALO, 1, LANES), jnp.float32)
    up, down = pl.pallas_call(
        pack_kernel,
        in_specs=[pl.BlockSpec(memory_space=pl.ANY)] * 2,
        out_specs=[pl.BlockSpec(memory_space=pltpu.VMEM)] * 2,
        out_shape=[out, out],
        scratch_shapes=[pltpu.VMEM((2, TILES, HALO, 1, LANES), jnp.int32), pltpu.SemaphoreType.DMA((4,))],
        compiler_params=pltpu.CompilerParams(vmem_limit_bytes=2 * MIB),
        name="pack",
    )(in_hbm(spectrum[..., None, :]), in_hbm(mask[..., None, :]))
    return up.reshape(SLOTS * SLOT, LANES), down.reshape(SLOTS * SLOT, LANES)


FETCH = 3
CHUNKS = NDIR // FETCH


def shifted(row, west):
    lane = lax.broadcasted_iota(jnp.int32, (8, LANES), 1)
    r = [pltpu.roll(v, 1 if west else LANES - 1, 1) for v in row]
    if west:
        return [jnp.where(lane == 0, r[j - 1], r[j]) for j in range(TILES)]
    return [jnp.where(lane == LANES - 1, r[(j + 1) % TILES], r[j]) for j in range(TILES)]


def interior_kernel(courant_ref, trig_ref, e_ref, mask_ref, out_ref, tile_ref, e_buf, out_buf, mask_s, sem, out_sem):
    fetch = lambda c: pltpu.make_async_copy(e_ref.at[pl.ds(c * FETCH, FETCH)], e_buf.at[pl.ds(c * FETCH, FETCH)], sem.at[c])
    put = lambda c: pltpu.make_async_copy(out_buf.at[:, pl.ds(c * FETCH, FETCH)], out_ref.at[:, pl.ds(c * FETCH, FETCH)], out_sem.at[c])
    for c in range(CHUNKS):
        fetch(c).start()
    sub = lax.broadcasted_iota(jnp.int32, (8, LANES), 0)
    mask_s[...] = mask_ref[...].astype(jnp.float32)

    def advance(south, west, first, i, carry):
        ds = [first + i * FETCH + u for u in range(FETCH)]
        many = range(FETCH)
        at, turn = (0, 1) if south else (7, 7)
        fetch(first // FETCH + i).wait()
        a = [courant_ref[0] * trig_ref[0, d] for d in ds]
        b = [courant_ref[0] * trig_ref[1, d] for d in ds]
        c = [1.0 - x - y for x, y in zip(a, b)]
        e = [[[e_buf[d, t, j] for j in range(TILES)] for t in range(8)] for d in ds]
        for u in many:
            for j in range(TILES):
                tile_ref[0 if south else 1, ds[u] - (0 if south else HALF), j] = e[u][at][j]
        for stage in range(SUBSTEPS):
            new = [[None] * 8 for _ in many]
            moved = [[[pltpu.roll(v, turn, 0) for v in row] for row in e[u]] for u in many]
            for t in range(8):
                for u in many:
                    x = shifted(e[u][t], west)
                    y = moved[u][t]
                    if t != at:
                        beyond = moved[u][t - 1 if south else t + 1]
                        y = [jnp.where(sub == at, beyond[j], y[j]) for j in range(TILES)]
                    new[u][t] = [mask_s[t, j] * (c[u] * e[u][t][j] + a[u] * x[j] + b[u] * y[j]) for j in range(TILES)]
            e = new
        odd, high = sub & 2 != 0, sub >= 4
        for u in many:
            for t in range(8):
                v = e[u][t]
                w = [
                    jnp.where(odd, pltpu.roll(v[1], 2, 0), v[0]),
                    jnp.where(odd, v[1], pltpu.roll(v[0], 6, 0)),
                    jnp.where(odd, pltpu.roll(v[3], 2, 0), v[2]),
                    jnp.where(odd, v[3], pltpu.roll(v[2], 6, 0)),
                ]
                out_buf[PLACE[4 * t], ds[u]] = jnp.where(high, pltpu.roll(w[2], 4, 0), w[0])
                out_buf[PLACE[4 * t + 1], ds[u]] = jnp.where(high, pltpu.roll(w[3], 4, 0), w[1])
                out_buf[PLACE[4 * t + 2], ds[u]] = jnp.where(high, w[2], pltpu.roll(w[0], 4, 0))
                out_buf[PLACE[4 * t + 3], ds[u]] = jnp.where(high, w[3], pltpu.roll(w[1], 4, 0))
        put(first // FETCH + i).start()
        return carry

    for q, (south, west) in enumerate(((True, True), (True, False), (False, False), (False, True))):
        lax.fori_loop(0, QUART // FETCH, functools.partial(advance, south, west, q * QUART), 0)
    for c in range(CHUNKS):
        put(c).wait()


def interior(spectrum, courant, mask):
    trig = np.stack([np.abs(COS), np.abs(SIN)])
    smem = pl.BlockSpec(memory_space=pltpu.SMEM)
    vmem = pl.BlockSpec(memory_space=pltpu.VMEM)
    hbm = pl.BlockSpec(memory_space=pl.ANY)
    return pl.pallas_call(
        interior_kernel,
        in_specs=[smem, smem, hbm, vmem],
        out_specs=[hbm, vmem],
        out_shape=[
            pltpu.HBM((32, NDIR, 8, LANES), jnp.float32),
            jax.ShapeDtypeStruct((2, HALF, TILES, 8, LANES), jnp.float32),
        ],
        scratch_shapes=[
            pltpu.VMEM((NDIR, ROWS // 8, TILES, 8, LANES), jnp.float32),
            pltpu.VMEM((32, NDIR, 8, LANES), jnp.float32),
            pltpu.VMEM((8, TILES, 8, LANES), jnp.float32),
            pltpu.SemaphoreType.DMA((CHUNKS,)),
            pltpu.SemaphoreType.DMA((CHUNKS,)),
        ],
        compiler_params=pltpu.CompilerParams(vmem_limit_bytes=12 * MIB),
        cost_estimate=pl.CostEstimate(flops=40_000_000, bytes_accessed=9_500_000, transcendentals=0),
        name="interior",
    )(courant, jnp.asarray(trig), in_hbm(spectrum), mask)


EDGE = 4


def edges_kernel(courant_ref, table_ref, tile_ref, mask_ref, south_ref, north_ref, p_in, p_ref, fixed, sem):
    del p_in
    sub = lax.broadcasted_iota(jnp.int32, (8, LANES), 0)
    flat_mask = mask_ref.reshape(ROWS * TILES, LANES)
    total = HALO + EDGE
    puts = []

    def eight(ref, start, n, stride):
        v = ref[pl.ds(start, n, stride=stride), :]
        return v if n == 8 else jnp.concatenate([v, jnp.zeros((8 - n, LANES), jnp.float32)], axis=0)

    for side, halo in enumerate((south_ref, north_ref)):
        south = side == 0
        tiles = tile_ref.at[side].reshape(HALF * ROWBLOCK, LANES)
        rows_out = fixed.at[side].reshape(2 * HALF * 8, LANES)
        own = lambda p: p - HALO if south else 7 - (p - HALO)
        sent = lambda p: p if south else HALO - 1 - p
        base = 0 if south else (ROWS // 8 - 1) * ROWBLOCK
        m = [None]
        for p in range(1, total):
            row = []
            for j in range(TILES):
                if p < HALO:
                    at = HALF * SLOT + j * HALO + sent(p)
                    row.append(halo[at : at + 1, :])
                else:
                    at = base + j * 8 + own(p)
                    row.append(flat_mask[at : at + 1, :].astype(jnp.float32))
            m.append(row)
        for g, n in ((0, 8), (8, 8), (16, 2)):
            a = courant_ref[0] * table_ref[2 * side, g : g + 8, :]
            b = courant_ref[0] * table_ref[2 * side + 1, g : g + 8, :]
            c = 1.0 - a - b
            e = []
            for p in range(total):
                if p < HALO:
                    e.append([eight(halo, g * SLOT + j * HALO + sent(p), n, SLOT) for j in range(TILES)])
                else:
                    e.append([eight(tiles, g * ROWBLOCK + j * 8 + own(p), n, ROWBLOCK) for j in range(TILES)])
            for k in range(SUBSTEPS):
                new = [None] * total
                for p in range(k + 1, total):
                    first = shifted(e[p], south) if g < 16 else None
                    second = shifted(e[p], not south) if g > 0 else None
                    if g == 0:
                        x = first
                    elif g == 16:
                        x = second
                    else:
                        x = [jnp.where(sub == 0, f, s) for f, s in zip(first, second)]
                    new[p] = [m[p][j] * (c * e[p][j] + a * x[j] + b * e[p - 1][j]) for j in range(TILES)]
                e = new
            for p in range(HALO, total):
                y = p - HALO if south else EDGE - 1 - (p - HALO)
                for j in range(TILES):
                    rows_out[pl.ds(((y // 2) * HALF + g) * 8 + 2 * j + y % 2, n, stride=8), :] = e[p][j][:n]
        for i in range(2):
            place = PLACE[i if south else 30 + i]
            put = pltpu.make_async_copy(
                fixed.at[side, i], p_ref.at[place, pl.ds(side * HALF, HALF)], sem.at[2 * side + i]
            )
            put.start()
            puts.append(put)
    for put in puts:
        put.wait()


def edges(tiles, courant, mask, from_south, from_north, inner):
    table = np.zeros((4, 24, LANES), np.float32)
    for side in range(2):
        ds = slice(side * HALF, (side + 1) * HALF)
        table[2 * side, :HALF] = np.abs(COS[ds])[:, None]
        table[2 * side + 1, :HALF] = np.abs(SIN[ds])[:, None]
    vmem = pl.BlockSpec(memory_space=pltpu.VMEM)
    hbm = pl.BlockSpec(memory_space=pl.ANY)
    return pl.pallas_call(
        edges_kernel,
        in_specs=[pl.BlockSpec(memory_space=pltpu.SMEM), vmem, vmem, vmem, vmem, vmem, hbm],
        out_specs=hbm,
        out_shape=pltpu.HBM(inner.shape, inner.dtype),
        scratch_shapes=[pltpu.VMEM((2, 2, HALF, 8, LANES), jnp.float32), pltpu.SemaphoreType.DMA((4,))],
        input_output_aliases={6: 0},
        compiler_params=pltpu.CompilerParams(vmem_limit_bytes=4 * MIB),
        name="edges",
    )(courant, jnp.asarray(table), tiles, mask, from_south, from_north, in_hbm(inner))


def pick_kernel(grp_ref, cells_ref, place_ref, p_ref, *out_refs):
    group = grp_ref[0]
    count = len(out_refs)
    lane = lax.broadcasted_iota(jnp.int32, (NDIR, LANES), 1)
    points = LANES // count
    for k, out in enumerate(out_refs):
        owner = lax.rem(group + k, count)
        nests = out.shape[0]

        def nest_body(n, carry):
            def point_body(p, acc):
                for u in range(8):
                    col = group * points + p * 8 + u
                    cell = lax.bitwise_and(cells_ref[owner * nests + n, col], ROWS * COLS - 1)
                    y = lax.shift_right_logical(cell, 9)
                    x = lax.bitwise_and(cell, COLS - 1)
                    row = place_ref[lax.shift_right_logical(y, 1)] * (NDIR * 8) + lax.shift_right_logical(x, 7) * 2 + lax.bitwise_and(y, 1)
                    got = p_ref[pl.ds(row, NDIR, stride=8), :]
                    turn = lax.bitwise_and(col - x, LANES - 1)
                    acc = jnp.where(lane == col, pltpu.roll(got, turn, 1), acc)
                return acc

            out[n] = lax.fori_loop(0, points // 8, point_body, jnp.zeros((NDIR, LANES), jnp.float32))
            return carry

        lax.fori_loop(0, nests, nest_body, 0)


def pick(group, cells, moved, count):
    nests = cells.shape[0] // count
    return pl.pallas_call(
        pick_kernel,
        in_specs=[
            pl.BlockSpec(memory_space=pltpu.SMEM),
            pl.BlockSpec(memory_space=pltpu.SMEM),
            pl.BlockSpec(memory_space=pltpu.SMEM),
            pl.BlockSpec(memory_space=pltpu.VMEM),
        ],
        out_specs=[pl.BlockSpec(memory_space=pltpu.VMEM)] * count,
        out_shape=[jax.ShapeDtypeStruct((nests, NDIR, LANES), jnp.float32)] * count,
        compiler_params=pltpu.CompilerParams(vmem_limit_bytes=8 * MIB),
        cost_estimate=pl.CostEstimate(flops=10_000_000, bytes_accessed=6_000_000, transcendentals=0),
        name="pick",
    )(group, cells, jnp.asarray(PLACE, jnp.int32), moved.reshape(32 * NDIR * 8, LANES))


def merge_kernel(*refs):
    *ins, out = refs
    nests = ins[0].shape[0]
    for n in range(nests):
        total = ins[0][n]
        for r in ins[1:]:
            total = total + r[n]
        out[pl.ds(n, NDIR, stride=nests), :] = total


def merge(parts):
    nests = parts[0].shape[0]
    out = pl.pallas_call(
        merge_kernel,
        out_shape=jax.ShapeDtypeStruct((NDIR * nests, LANES), jnp.float32),
        compiler_params=pltpu.CompilerParams(vmem_limit_bytes=4 * MIB),
        name="merge",
    )(*parts)
    return out.reshape(NDIR, nests, LANES)


FCHUNK = 4
NCHUNK = NFREQ // FCHUNK


def source_kernel(recv_ref, u_ref, v_ref, out_ref, buf, outbuf, sem, osem):
    put = lambda c: pltpu.make_async_copy(
        outbuf.at[pl.ds(c * FCHUNK, FCHUNK)], out_ref.at[pl.ds(c * FCHUNK, FCHUNK)], osem.at[c]
    )
    fetch = lambda c: pltpu.make_async_copy(recv_ref.at[pl.ds(c * FCHUNK, FCHUNK)], buf.at[pl.ds(c * FCHUNK, FCHUNK)], sem.at[c])
    for c in range(NCHUNK):
        fetch(c).start()
    total = jnp.zeros((8, LANES), jnp.float32)
    weighted = jnp.zeros((8, LANES), jnp.float32)
    for p, f in enumerate(ORDER):
        if p % FCHUNK == 0:
            fetch(p // FCHUNK).wait()
        s = jnp.sum(buf[p], axis=0)
        total = total + s
        weighted = weighted + s * float(SCALE[f] * SCALE[f])
    m0 = total * (1.0 / (NFREQ * NDIR))
    q = weighted * (1.0 / (NFREQ * NDIR))
    ratio = jnp.maximum(m0, 0.05) / jnp.maximum(q, 0.1)
    steep = m0 / 0.3
    base = ratio * (steep * steep)
    u = u_ref[...]
    v = v_ref[...]

    for c in range(NCHUNK):
        fs = range(c * FCHUNK, (c + 1) * FCHUNK)
        loss = [base * float(0.1 * SCALE[f] ** 3 * LOG2E) for f in fs]
        for d in range(NDIR):
            proj = u * float(COS[d]) + v * float(SIN[d])
            for i, f in enumerate(fs):
                gain = jnp.maximum(proj * float(0.05 * SCALE[f] ** 2 * LOG2E) - float(0.05 * SCALE[f] * LOG2E), 0.0)
                outbuf[f, d] = buf[PLACE[f], d] * jnp.exp2(gain - loss[i])
        put(c).start()
    for c in range(NCHUNK):
        put(c).wait()


def sources(recv, wind_u, wind_v):
    tile = lambda w: w.reshape(2, TILES, LANES).transpose(1, 0, 2).reshape(8, LANES)
    shape = (NFREQ, NDIR, 8, LANES)
    out = pl.pallas_call(
        source_kernel,
        in_specs=[pl.BlockSpec(memory_space=pl.ANY)] + [pl.BlockSpec(memory_space=pltpu.VMEM)] * 2,
        out_specs=pl.BlockSpec(memory_space=pltpu.HBM),
        out_shape=jax.ShapeDtypeStruct(shape, jnp.float32),
        scratch_shapes=[
            pltpu.VMEM(shape, jnp.float32),
            pltpu.VMEM(shape, jnp.float32),
            pltpu.SemaphoreType.DMA((NCHUNK,)),
            pltpu.SemaphoreType.DMA((NCHUNK,)),
        ],
        compiler_params=pltpu.CompilerParams(vmem_limit_bytes=12 * MIB),
        name="sources",
    )(in_hbm(recv), tile(wind_u), tile(wind_v))
    out = out.reshape(NFREQ, NDIR, TILES, 2, LANES).transpose(0, 1, 3, 2, 4)
    return out.reshape(NFREQ, NDIR, 1, 2, COLS)


def per_device(spectrum, courant, sea_mask, wind_u, wind_v, boundary_cells):
    size = lax.axis_size("grp")
    group = lax.axis_index("grp").astype(jnp.int32).reshape(1)
    block = tiled(spectrum.reshape(NDIR, ROWS, COLS))
    mask = tiled(sea_mask.reshape(ROWS, COLS))
    up, down = pack(block, mask)
    from_south = lax.ppermute(up, "grp", [(i, i + 1) for i in range(size - 1)])
    from_north = lax.ppermute(down, "grp", [(i + 1, i) for i in range(size - 1)])
    inner, tiles = interior(block, courant, mask)
    result = edges(tiles, courant, mask, from_south, from_north, inner)
    moved = lax.all_to_all(result, "comp", split_axis=0, concat_axis=0, axis_index_groups=[list(ORDER)], tiled=True)
    picked = pick(group, boundary_cells, result, size)
    parts = [picked[0]]
    for k in range(1, size):
        parts.append(lax.ppermute(picked[k], "grp", [(i, (i + k) % size) for i in range(size)]))
    boundary = merge(parts)[None]
    updated = sources(moved, wind_u.reshape(2, COLS), wind_v.reshape(2, COLS))
    return updated, boundary


def solution(mesh):
    placed = (
        P("comp", None, "grp", None, None),
        P("comp"),
        P("grp", None, None),
        P("grp", "comp", None),
        P("grp", "comp", None),
        P(),
    )
    return jax.shard_map(
        per_device,
        mesh=mesh,
        in_specs=placed,
        out_specs=(P(None, None, "grp", "comp", None), P("comp", None, "grp", None)),
        check_vma=False,
    )
```

```python
import functools

import jax
import jax.numpy as jnp
import numpy as np
from jax import lax
from jax.experimental import pallas as pl
from jax.experimental.pallas import tpu as pltpu
from jax.sharding import PartitionSpec as P

NDIR = 36
NFREQ = 32
SUBSTEPS = 3
HALF = NDIR // 2
QUART = NDIR // 4
ROWS = 64
COLS = 512
LANES = 128
TILES = COLS // LANES
HALO = 3
SLOTS = HALF + 2
SLOT = TILES * HALO
ROWBLOCK = TILES * 8
MIB = 1024 * 1024

THETA = (2.0 * np.pi * np.arange(NDIR) / NDIR).astype(np.float32)
COS = np.cos(THETA).astype(np.float32)
SIN = np.sin(THETA).astype(np.float32)
SCALE = (0.3 * np.float32(1.1) ** np.arange(NFREQ, dtype=np.float32)).astype(np.float32)
LOG2E = 1.4426950408889634

ORDER = (15, 27, 28, 26, 22, 18, 24, 3, 9, 25, 6, 13, 7, 31, 20, 12, 1, 17, 23, 2, 30, 14, 16, 10, 0, 21, 5, 4, 8, 11, 19, 29)
PLACE = tuple(int(p) for p in np.argsort(ORDER))


def tiled(value):
    lead = value.shape[:-2]
    n = len(lead)
    value = value.reshape(*lead, ROWS // 8, 8, TILES, LANES)
    return value.transpose(*range(n), n, n + 2, n + 1, n + 3)


def in_hbm(value):
    return pltpu.with_memory_space_constraint(value, pltpu.HBM)


def pack_kernel(grp_ref, spectrum_ref, mask_ref, out_ref, packed, mask_s, sem):
    size = out_ref.shape[0]
    group = grp_ref[0]
    sides = (
        (lax.rem(group + 1, size), 0, ROWS // 8 - 1, 8 - HALO),
        (lax.rem(group + size - 1, size), HALF, 0, 0),
    )
    rows, masks, puts = [], [], []
    for side, (slot, d, tile, low) in enumerate(sides):
        near = pl.ds(low, HALO)
        rows.append(
            pltpu.make_async_copy(
                spectrum_ref.at[pl.ds(d, HALF), tile, :, near], packed.at[side, pl.ds(0, HALF)], sem.at[side]
            )
        )
        masks.append(pltpu.make_async_copy(mask_ref.at[tile, :, near], mask_s.at[side], sem.at[2 + side]))
        puts.append(pltpu.make_async_copy(packed.at[side], out_ref.at[slot], sem.at[4 + side]))
    for copy in rows + masks:
        copy.start()
    for side in range(2):
        masks[side].wait()
        packed[side, HALF] = mask_s[side].astype(jnp.float32)
        packed[side, HALF + 1] = jnp.zeros((TILES, HALO, 1, LANES), jnp.float32)
    for side in range(2):
        rows[side].wait()
        puts[side].start()
    for copy in puts:
        copy.wait()


def pack(group, spectrum, mask, size):
    out = pl.pallas_call(
        pack_kernel,
        in_specs=[pl.BlockSpec(memory_space=pltpu.SMEM)] + [pl.BlockSpec(memory_space=pl.ANY)] * 2,
        out_specs=pl.BlockSpec(memory_space=pl.ANY),
        out_shape=pltpu.HBM((size, SLOTS, TILES, HALO, 1, LANES), jnp.float32),
        scratch_shapes=[
            pltpu.VMEM((2, SLOTS, TILES, HALO, 1, LANES), jnp.float32),
            pltpu.VMEM((2, TILES, HALO, 1, LANES), jnp.int32),
            pltpu.SemaphoreType.DMA((6,)),
        ],
        compiler_params=pltpu.CompilerParams(vmem_limit_bytes=2 * MIB),
        name="pack",
    )(group, in_hbm(spectrum[..., None, :]), in_hbm(mask[..., None, :]))
    return out.reshape(size, SLOTS * SLOT, LANES)


FETCH = 3
CHUNKS = NDIR // FETCH


def shifted(row, west):
    lane = lax.broadcasted_iota(jnp.int32, (8, LANES), 1)
    r = [pltpu.roll(v, 1 if west else LANES - 1, 1) for v in row]
    if west:
        return [jnp.where(lane == 0, r[j - 1], r[j]) for j in range(TILES)]
    return [jnp.where(lane == LANES - 1, r[(j + 1) % TILES], r[j]) for j in range(TILES)]


def interior_kernel(courant_ref, trig_ref, e_ref, mask_ref, out_ref, tile_ref, e_buf, out_buf, mask_s, sem, out_sem):
    fetch = lambda c: pltpu.make_async_copy(e_ref.at[pl.ds(c * FETCH, FETCH)], e_buf.at[pl.ds(c * FETCH, FETCH)], sem.at[c])
    put = lambda c: pltpu.make_async_copy(out_buf.at[:, pl.ds(c * FETCH, FETCH)], out_ref.at[:, pl.ds(c * FETCH, FETCH)], out_sem.at[c])
    for c in range(CHUNKS):
        fetch(c).start()
    sub = lax.broadcasted_iota(jnp.int32, (8, LANES), 0)
    mask_s[...] = mask_ref[...].astype(jnp.float32)

    def advance(south, west, first, i, carry):
        ds = [first + i * FETCH + u for u in range(FETCH)]
        many = range(FETCH)
        at, turn = (0, 1) if south else (7, 7)
        fetch(first // FETCH + i).wait()
        a = [courant_ref[0] * trig_ref[0, d] for d in ds]
        b = [courant_ref[0] * trig_ref[1, d] for d in ds]
        c = [1.0 - x - y for x, y in zip(a, b)]
        e = [[[e_buf[d, t, j] for j in range(TILES)] for t in range(8)] for d in ds]
        for u in many:
            for j in range(TILES):
                tile_ref[0 if south else 1, ds[u] - (0 if south else HALF), j] = e[u][at][j]
        for stage in range(SUBSTEPS):
            new = [[None] * 8 for _ in many]
            moved = [[[pltpu.roll(v, turn, 0) for v in row] for row in e[u]] for u in many]
            for t in range(8):
                for u in many:
                    x = shifted(e[u][t], west)
                    y = moved[u][t]
                    if t != at:
                        beyond = moved[u][t - 1 if south else t + 1]
                        y = [jnp.where(sub == at, beyond[j], y[j]) for j in range(TILES)]
                    new[u][t] = [mask_s[t, j] * (c[u] * e[u][t][j] + a[u] * x[j] + b[u] * y[j]) for j in range(TILES)]
            e = new
        odd, high = sub & 2 != 0, sub >= 4
        for u in many:
            for t in range(8):
                v = e[u][t]
                w = [
                    jnp.where(odd, pltpu.roll(v[1], 2, 0), v[0]),
                    jnp.where(odd, v[1], pltpu.roll(v[0], 6, 0)),
                    jnp.where(odd, pltpu.roll(v[3], 2, 0), v[2]),
                    jnp.where(odd, v[3], pltpu.roll(v[2], 6, 0)),
                ]
                out_buf[PLACE[4 * t], ds[u]] = jnp.where(high, pltpu.roll(w[2], 4, 0), w[0])
                out_buf[PLACE[4 * t + 1], ds[u]] = jnp.where(high, pltpu.roll(w[3], 4, 0), w[1])
                out_buf[PLACE[4 * t + 2], ds[u]] = jnp.where(high, w[2], pltpu.roll(w[0], 4, 0))
                out_buf[PLACE[4 * t + 3], ds[u]] = jnp.where(high, w[3], pltpu.roll(w[1], 4, 0))
        put(first // FETCH + i).start()
        return carry

    for q, (south, west) in enumerate(((True, True), (True, False), (False, False), (False, True))):
        lax.fori_loop(0, QUART // FETCH, functools.partial(advance, south, west, q * QUART), 0)
    for c in range(CHUNKS):
        put(c).wait()


def interior(spectrum, courant, mask):
    trig = np.stack([np.abs(COS), np.abs(SIN)])
    smem = pl.BlockSpec(memory_space=pltpu.SMEM)
    vmem = pl.BlockSpec(memory_space=pltpu.VMEM)
    hbm = pl.BlockSpec(memory_space=pl.ANY)
    return pl.pallas_call(
        interior_kernel,
        in_specs=[smem, smem, hbm, vmem],
        out_specs=[hbm, vmem],
        out_shape=[
            pltpu.HBM((32, NDIR, 8, LANES), jnp.float32),
            jax.ShapeDtypeStruct((2, HALF, TILES, 8, LANES), jnp.float32),
        ],
        scratch_shapes=[
            pltpu.VMEM((NDIR, ROWS // 8, TILES, 8, LANES), jnp.float32),
            pltpu.VMEM((32, NDIR, 8, LANES), jnp.float32),
            pltpu.VMEM((8, TILES, 8, LANES), jnp.float32),
            pltpu.SemaphoreType.DMA((CHUNKS,)),
            pltpu.SemaphoreType.DMA((CHUNKS,)),
        ],
        compiler_params=pltpu.CompilerParams(vmem_limit_bytes=12 * MIB),
        cost_estimate=pl.CostEstimate(flops=40_000_000, bytes_accessed=9_500_000, transcendentals=0),
        name="interior",
    )(courant, jnp.asarray(trig), in_hbm(spectrum), mask)


EDGE = 4


def edges_kernel(grp_ref, courant_ref, table_ref, tile_ref, mask_ref, halo_ref, p_in, p_ref, fixed, sem):
    del p_in
    sub = lax.broadcasted_iota(jnp.int32, (8, LANES), 0)
    flat_mask = mask_ref.reshape(ROWS * TILES, LANES)
    total = HALO + EDGE
    puts = []

    def eight(ref, start, n, stride):
        v = ref[pl.ds(start, n, stride=stride), :]
        return v if n == 8 else jnp.concatenate([v, jnp.zeros((8 - n, LANES), jnp.float32)], axis=0)

    size = halo_ref.shape[0]
    group = grp_ref[0]
    neighbours = (
        (lax.rem(group + size - 1, size), group > 0),
        (lax.rem(group + 1, size), group < size - 1),
    )
    for side, (source, inside) in enumerate(neighbours):
        halo = halo_ref.at[source]
        keep = jnp.where(inside, 1.0, 0.0)
        south = side == 0
        tiles = tile_ref.at[side].reshape(HALF * ROWBLOCK, LANES)
        rows_out = fixed.at[side].reshape(2 * HALF * 8, LANES)
        own = lambda p: p - HALO if south else 7 - (p - HALO)
        sent = lambda p: p if south else HALO - 1 - p
        base = 0 if south else (ROWS // 8 - 1) * ROWBLOCK
        m = [None]
        for p in range(1, total):
            row = []
            for j in range(TILES):
                if p < HALO:
                    at = HALF * SLOT + j * HALO + sent(p)
                    row.append(halo[at : at + 1, :])
                else:
                    at = base + j * 8 + own(p)
                    row.append(flat_mask[at : at + 1, :].astype(jnp.float32))
            m.append(row)
        for g, n in ((0, 8), (8, 8), (16, 2)):
            a = courant_ref[0] * table_ref[2 * side, g : g + 8, :]
            b = courant_ref[0] * table_ref[2 * side + 1, g : g + 8, :]
            c = 1.0 - a - b
            e = []
            for p in range(total):
                if p < HALO:
                    e.append([keep * eight(halo, g * SLOT + j * HALO + sent(p), n, SLOT) for j in range(TILES)])
                else:
                    e.append([eight(tiles, g * ROWBLOCK + j * 8 + own(p), n, ROWBLOCK) for j in range(TILES)])
            for k in range(SUBSTEPS):
                new = [None] * total
                for p in range(k + 1, total):
                    first = shifted(e[p], south) if g < 16 else None
                    second = shifted(e[p], not south) if g > 0 else None
                    if g == 0:
                        x = first
                    elif g == 16:
                        x = second
                    else:
                        x = [jnp.where(sub == 0, f, s) for f, s in zip(first, second)]
                    new[p] = [m[p][j] * (c * e[p][j] + a * x[j] + b * e[p - 1][j]) for j in range(TILES)]
                e = new
            for p in range(HALO, total):
                y = p - HALO if south else EDGE - 1 - (p - HALO)
                for j in range(TILES):
                    rows_out[pl.ds(((y // 2) * HALF + g) * 8 + 2 * j + y % 2, n, stride=8), :] = e[p][j][:n]
        for i in range(2):
            place = PLACE[i if south else 30 + i]
            put = pltpu.make_async_copy(
                fixed.at[side, i], p_ref.at[place, pl.ds(side * HALF, HALF)], sem.at[2 * side + i]
            )
            put.start()
            puts.append(put)
    for put in puts:
        put.wait()


def edges(group, tiles, courant, mask, halos, inner):
    table = np.zeros((4, 24, LANES), np.float32)
    for side in range(2):
        ds = slice(side * HALF, (side + 1) * HALF)
        table[2 * side, :HALF] = np.abs(COS[ds])[:, None]
        table[2 * side + 1, :HALF] = np.abs(SIN[ds])[:, None]
    vmem = pl.BlockSpec(memory_space=pltpu.VMEM)
    hbm = pl.BlockSpec(memory_space=pl.ANY)
    return pl.pallas_call(
        edges_kernel,
        in_specs=[pl.BlockSpec(memory_space=pltpu.SMEM)] * 2 + [vmem, vmem, vmem, vmem, hbm],
        out_specs=hbm,
        out_shape=pltpu.HBM(inner.shape, inner.dtype),
        scratch_shapes=[pltpu.VMEM((2, 2, HALF, 8, LANES), jnp.float32), pltpu.SemaphoreType.DMA((4,))],
        input_output_aliases={6: 0},
        compiler_params=pltpu.CompilerParams(vmem_limit_bytes=4 * MIB),
        name="edges",
    )(group, courant, jnp.asarray(table), tiles, mask, halos, in_hbm(inner))


def pick_kernel(grp_ref, cells_ref, place_ref, p_ref, *out_refs):
    group = grp_ref[0]
    count = len(out_refs)
    lane = lax.broadcasted_iota(jnp.int32, (NDIR, LANES), 1)
    points = LANES // count
    for k, out in enumerate(out_refs):
        owner = lax.rem(group + k, count)
        nests = out.shape[0]

        def nest_body(n, carry):
            def point_body(p, acc):
                for u in range(8):
                    col = group * points + p * 8 + u
                    cell = lax.bitwise_and(cells_ref[owner * nests + n, col], ROWS * COLS - 1)
                    y = lax.shift_right_logical(cell, 9)
                    x = lax.bitwise_and(cell, COLS - 1)
                    row = place_ref[lax.shift_right_logical(y, 1)] * (NDIR * 8) + lax.shift_right_logical(x, 7) * 2 + lax.bitwise_and(y, 1)
                    got = p_ref[pl.ds(row, NDIR, stride=8), :]
                    turn = lax.bitwise_and(col - x, LANES - 1)
                    acc = jnp.where(lane == col, pltpu.roll(got, turn, 1), acc)
                return acc

            out[n] = lax.fori_loop(0, points // 8, point_body, jnp.zeros((NDIR, LANES), jnp.float32))
            return carry

        lax.fori_loop(0, nests, nest_body, 0)


def pick(group, cells, moved, count):
    nests = cells.shape[0] // count
    return pl.pallas_call(
        pick_kernel,
        in_specs=[
            pl.BlockSpec(memory_space=pltpu.SMEM),
            pl.BlockSpec(memory_space=pltpu.SMEM),
            pl.BlockSpec(memory_space=pltpu.SMEM),
            pl.BlockSpec(memory_space=pltpu.VMEM),
        ],
        out_specs=[pl.BlockSpec(memory_space=pltpu.VMEM)] * count,
        out_shape=[jax.ShapeDtypeStruct((nests, NDIR, LANES), jnp.float32)] * count,
        compiler_params=pltpu.CompilerParams(vmem_limit_bytes=8 * MIB),
        cost_estimate=pl.CostEstimate(flops=10_000_000, bytes_accessed=6_000_000, transcendentals=0),
        name="pick",
    )(group, cells, jnp.asarray(PLACE, jnp.int32), moved.reshape(32 * NDIR * 8, LANES))


def merge_kernel(*refs):
    *ins, out = refs
    nests = ins[0].shape[0]
    for n in range(nests):
        total = ins[0][n]
        for r in ins[1:]:
            total = total + r[n]
        out[pl.ds(n, NDIR, stride=nests), :] = total


def merge(parts):
    nests = parts[0].shape[0]
    out = pl.pallas_call(
        merge_kernel,
        out_shape=jax.ShapeDtypeStruct((NDIR * nests, LANES), jnp.float32),
        compiler_params=pltpu.CompilerParams(vmem_limit_bytes=4 * MIB),
        name="merge",
    )(*parts)
    return out.reshape(NDIR, nests, LANES)


FCHUNK = 4
NCHUNK = NFREQ // FCHUNK


def source_kernel(recv_ref, u_ref, v_ref, out_ref, buf, outbuf, sem, osem):
    put = lambda c: pltpu.make_async_copy(
        outbuf.at[pl.ds(c * FCHUNK, FCHUNK)], out_ref.at[pl.ds(c * FCHUNK, FCHUNK)], osem.at[c]
    )
    fetch = lambda c: pltpu.make_async_copy(recv_ref.at[pl.ds(c * FCHUNK, FCHUNK)], buf.at[pl.ds(c * FCHUNK, FCHUNK)], sem.at[c])
    for c in range(NCHUNK):
        fetch(c).start()
    total = jnp.zeros((8, LANES), jnp.float32)
    weighted = jnp.zeros((8, LANES), jnp.float32)
    for p, f in enumerate(ORDER):
        if p % FCHUNK == 0:
            fetch(p // FCHUNK).wait()
        s = jnp.sum(buf[p], axis=0)
        total = total + s
        weighted = weighted + s * float(SCALE[f] * SCALE[f])
    m0 = total * (1.0 / (NFREQ * NDIR))
    q = weighted * (1.0 / (NFREQ * NDIR))
    ratio = jnp.maximum(m0, 0.05) / jnp.maximum(q, 0.1)
    steep = m0 / 0.3
    base = ratio * (steep * steep)
    u = u_ref[...]
    v = v_ref[...]

    for c in range(NCHUNK):
        fs = range(c * FCHUNK, (c + 1) * FCHUNK)
        loss = [base * float(0.1 * SCALE[f] ** 3 * LOG2E) for f in fs]
        for d in range(NDIR):
            proj = u * float(COS[d]) + v * float(SIN[d])
            for i, f in enumerate(fs):
                gain = jnp.maximum(proj * float(0.05 * SCALE[f] ** 2 * LOG2E) - float(0.05 * SCALE[f] * LOG2E), 0.0)
                outbuf[f, d] = buf[PLACE[f], d] * jnp.exp2(gain - loss[i])
        put(c).start()
    for c in range(NCHUNK):
        put(c).wait()


def sources(recv, wind_u, wind_v):
    tile = lambda w: w.reshape(2, TILES, LANES).transpose(1, 0, 2).reshape(8, LANES)
    shape = (NFREQ, NDIR, 8, LANES)
    out = pl.pallas_call(
        source_kernel,
        in_specs=[pl.BlockSpec(memory_space=pl.ANY)] + [pl.BlockSpec(memory_space=pltpu.VMEM)] * 2,
        out_specs=pl.BlockSpec(memory_space=pltpu.HBM),
        out_shape=jax.ShapeDtypeStruct(shape, jnp.float32),
        scratch_shapes=[
            pltpu.VMEM(shape, jnp.float32),
            pltpu.VMEM(shape, jnp.float32),
            pltpu.SemaphoreType.DMA((NCHUNK,)),
            pltpu.SemaphoreType.DMA((NCHUNK,)),
        ],
        compiler_params=pltpu.CompilerParams(vmem_limit_bytes=12 * MIB),
        name="sources",
    )(in_hbm(recv), tile(wind_u), tile(wind_v))
    out = out.reshape(NFREQ, NDIR, TILES, 2, LANES).transpose(0, 1, 3, 2, 4)
    return out.reshape(NFREQ, NDIR, 1, 2, COLS)


def per_device(spectrum, courant, sea_mask, wind_u, wind_v, boundary_cells):
    size = lax.axis_size("grp")
    group = lax.axis_index("grp").astype(jnp.int32).reshape(1)
    block = tiled(spectrum.reshape(NDIR, ROWS, COLS))
    mask = tiled(sea_mask.reshape(ROWS, COLS))
    halos = pack(group, block, mask, size)
    halos = lax.all_to_all(halos, "grp", split_axis=0, concat_axis=0, tiled=True)
    inner, tiles = interior(block, courant, mask)
    result = edges(group, tiles, courant, mask, halos, inner)
    moved = lax.all_to_all(result, "comp", split_axis=0, concat_axis=0, axis_index_groups=[list(ORDER)], tiled=True)
    picked = pick(group, boundary_cells, result, size)
    parts = [picked[0]]
    for k in range(1, size):
        parts.append(lax.ppermute(picked[k], "grp", [(i, (i + k) % size) for i in range(size)]))
    boundary = merge(parts)[None]
    updated = sources(moved, wind_u.reshape(2, COLS), wind_v.reshape(2, COLS))
    return updated, boundary


def solution(mesh):
    placed = (
        P("comp", None, "grp", None, None),
        P("comp"),
        P("grp", None, None),
        P("grp", "comp", None),
        P("grp", "comp", None),
        P(),
    )
    return jax.shard_map(
        per_device,
        mesh=mesh,
        in_specs=placed,
        out_specs=(P(None, None, "grp", "comp", None), P("comp", None, "grp", None)),
        check_vma=False,
    )
```

```python
import functools

import jax
import jax.numpy as jnp
import numpy as np
from jax import lax
from jax.experimental import pallas as pl
from jax.experimental.pallas import tpu as pltpu
from jax.sharding import PartitionSpec as P

NDIR = 36
NFREQ = 32
SUBSTEPS = 3
HALF = NDIR // 2
QUART = NDIR // 4
ROWS = 64
COLS = 512
LANES = 128
TILES = COLS // LANES
HALO = 3
SLOTS = HALF + 2
SLOT = TILES * HALO
ROWBLOCK = TILES * 8
MIB = 1024 * 1024

THETA = (2.0 * np.pi * np.arange(NDIR) / NDIR).astype(np.float32)
COS = np.cos(THETA).astype(np.float32)
SIN = np.sin(THETA).astype(np.float32)
SCALE = (0.3 * np.float32(1.1) ** np.arange(NFREQ, dtype=np.float32)).astype(np.float32)
LOG2E = 1.4426950408889634

ORDER = (15, 27, 28, 26, 22, 18, 24, 3, 9, 25, 6, 13, 7, 31, 20, 12, 1, 17, 23, 2, 30, 14, 16, 10, 0, 21, 5, 4, 8, 11, 19, 29)
PLACE = tuple(int(p) for p in np.argsort(ORDER))


def tiled(value):
    lead = value.shape[:-2]
    n = len(lead)
    value = value.reshape(*lead, ROWS // 8, 8, TILES, LANES)
    return value.transpose(*range(n), n, n + 2, n + 1, n + 3)


def in_hbm(value):
    return pltpu.with_memory_space_constraint(value, pltpu.HBM)


def pack_kernel(grp_ref, spectrum_ref, mask_ref, out_ref, packed, mask_s, sem):
    size = out_ref.shape[0]
    group = grp_ref[0]
    sides = (
        (lax.rem(group + 1, size), 0, ROWS // 8 - 1, 8 - HALO),
        (lax.rem(group + size - 1, size), HALF, 0, 0),
    )
    rows, masks, puts = [], [], []
    for side, (slot, d, tile, low) in enumerate(sides):
        near = pl.ds(low, HALO)
        rows.append(
            pltpu.make_async_copy(
                spectrum_ref.at[pl.ds(d, HALF), tile, :, near], packed.at[side, pl.ds(0, HALF)], sem.at[side]
            )
        )
        masks.append(pltpu.make_async_copy(mask_ref.at[tile, :, near], mask_s.at[side], sem.at[2 + side]))
        puts.append(pltpu.make_async_copy(packed.at[side], out_ref.at[slot], sem.at[4 + side]))
    for copy in rows + masks:
        copy.start()
    for side in range(2):
        masks[side].wait()
        packed[side, HALF] = mask_s[side].astype(jnp.float32)
        packed[side, HALF + 1] = jnp.zeros((TILES, HALO, 1, LANES), jnp.float32)
    for side in range(2):
        rows[side].wait()
        puts[side].start()
    for copy in puts:
        copy.wait()


def pack(group, spectrum, mask, size):
    out = pl.pallas_call(
        pack_kernel,
        in_specs=[pl.BlockSpec(memory_space=pltpu.SMEM)] + [pl.BlockSpec(memory_space=pl.ANY)] * 2,
        out_specs=pl.BlockSpec(memory_space=pl.ANY),
        out_shape=pltpu.HBM((size, SLOTS, TILES, HALO, 1, LANES), jnp.float32),
        scratch_shapes=[
            pltpu.VMEM((2, SLOTS, TILES, HALO, 1, LANES), jnp.float32),
            pltpu.VMEM((2, TILES, HALO, 1, LANES), jnp.int32),
            pltpu.SemaphoreType.DMA((6,)),
        ],
        compiler_params=pltpu.CompilerParams(vmem_limit_bytes=2 * MIB),
        name="pack",
    )(group, in_hbm(spectrum[..., None, :]), in_hbm(mask[..., None, :]))
    return out.reshape(size, SLOTS * SLOT, LANES)


FETCH = 3
CHUNKS = NDIR // FETCH


def shifted(row, west):
    lane = lax.broadcasted_iota(jnp.int32, (8, LANES), 1)
    r = [pltpu.roll(v, 1 if west else LANES - 1, 1) for v in row]
    if west:
        return [jnp.where(lane == 0, r[j - 1], r[j]) for j in range(TILES)]
    return [jnp.where(lane == LANES - 1, r[(j + 1) % TILES], r[j]) for j in range(TILES)]


def interior_kernel(courant_ref, trig_ref, e_ref, mask_ref, out_ref, tile_ref, e_buf, out_buf, mask_s, sem, out_sem):
    fetch = lambda c: pltpu.make_async_copy(e_ref.at[pl.ds(c * FETCH, FETCH)], e_buf.at[pl.ds(c * FETCH, FETCH)], sem.at[c])
    put = lambda c: pltpu.make_async_copy(out_buf.at[:, pl.ds(c * FETCH, FETCH)], out_ref.at[:, pl.ds(c * FETCH, FETCH)], out_sem.at[c])
    for c in range(CHUNKS):
        fetch(c).start()
    sub = lax.broadcasted_iota(jnp.int32, (8, LANES), 0)
    mask_s[...] = mask_ref[...].astype(jnp.float32)

    def advance(south, west, first, i, carry):
        ds = [first + i * FETCH + u for u in range(FETCH)]
        many = range(FETCH)
        at, turn = (0, 1) if south else (7, 7)
        fetch(first // FETCH + i).wait()
        a = [courant_ref[0] * trig_ref[0, d] for d in ds]
        b = [courant_ref[0] * trig_ref[1, d] for d in ds]
        c = [1.0 - x - y for x, y in zip(a, b)]
        e = [[[e_buf[d, t, j] for j in range(TILES)] for t in range(8)] for d in ds]
        for u in many:
            for j in range(TILES):
                tile_ref[0 if south else 1, ds[u] - (0 if south else HALF), j] = e[u][at][j]
        for stage in range(SUBSTEPS):
            new = [[None] * 8 for _ in many]
            moved = [[[pltpu.roll(v, turn, 0) for v in row] for row in e[u]] for u in many]
            for u in many:
                for t in range(8):
                    x = shifted(e[u][t], west)
                    y = moved[u][t]
                    if t != at:
                        beyond = moved[u][t - 1 if south else t + 1]
                        y = [jnp.where(sub == at, beyond[j], y[j]) for j in range(TILES)]
                    new[u][t] = [mask_s[t, j] * (c[u] * e[u][t][j] + a[u] * x[j] + b[u] * y[j]) for j in range(TILES)]
            e = new
        odd, high = sub & 2 != 0, sub >= 4
        for u in many:
            for t in range(8):
                v = e[u][t]
                w = [
                    jnp.where(odd, pltpu.roll(v[1], 2, 0), v[0]),
                    jnp.where(odd, v[1], pltpu.roll(v[0], 6, 0)),
                    jnp.where(odd, pltpu.roll(v[3], 2, 0), v[2]),
                    jnp.where(odd, v[3], pltpu.roll(v[2], 6, 0)),
                ]
                out_buf[PLACE[4 * t], ds[u]] = jnp.where(high, pltpu.roll(w[2], 4, 0), w[0])
                out_buf[PLACE[4 * t + 1], ds[u]] = jnp.where(high, pltpu.roll(w[3], 4, 0), w[1])
                out_buf[PLACE[4 * t + 2], ds[u]] = jnp.where(high, w[2], pltpu.roll(w[0], 4, 0))
                out_buf[PLACE[4 * t + 3], ds[u]] = jnp.where(high, w[3], pltpu.roll(w[1], 4, 0))
        put(first // FETCH + i).start()
        return carry

    for q, (south, west) in enumerate(((True, True), (True, False), (False, False), (False, True))):
        lax.fori_loop(0, QUART // FETCH, functools.partial(advance, south, west, q * QUART), 0)
    for c in range(CHUNKS):
        put(c).wait()


def interior(spectrum, courant, mask):
    trig = np.stack([np.abs(COS), np.abs(SIN)])
    smem = pl.BlockSpec(memory_space=pltpu.SMEM)
    vmem = pl.BlockSpec(memory_space=pltpu.VMEM)
    hbm = pl.BlockSpec(memory_space=pl.ANY)
    return pl.pallas_call(
        interior_kernel,
        in_specs=[smem, smem, hbm, vmem],
        out_specs=[hbm, vmem],
        out_shape=[
            pltpu.HBM((32, NDIR, 8, LANES), jnp.float32),
            jax.ShapeDtypeStruct((2, HALF, TILES, 8, LANES), jnp.float32),
        ],
        scratch_shapes=[
            pltpu.VMEM((NDIR, ROWS // 8, TILES, 8, LANES), jnp.float32),
            pltpu.VMEM((32, NDIR, 8, LANES), jnp.float32),
            pltpu.VMEM((8, TILES, 8, LANES), jnp.float32),
            pltpu.SemaphoreType.DMA((CHUNKS,)),
            pltpu.SemaphoreType.DMA((CHUNKS,)),
        ],
        compiler_params=pltpu.CompilerParams(vmem_limit_bytes=12 * MIB),
        cost_estimate=pl.CostEstimate(flops=40_000_000, bytes_accessed=9_500_000, transcendentals=0),
        name="interior",
    )(courant, jnp.asarray(trig), in_hbm(spectrum), mask)


EDGE = 4


def edges_kernel(grp_ref, courant_ref, table_ref, tile_ref, mask_ref, halo_ref, p_in, p_ref, fixed, sem):
    del p_in
    sub = lax.broadcasted_iota(jnp.int32, (8, LANES), 0)
    flat_mask = mask_ref.reshape(ROWS * TILES, LANES)
    total = HALO + EDGE
    puts = []

    def eight(ref, start, n, stride):
        if n == 8:
            return ref[pl.ds(start, n, stride=stride), :]
        rows = [ref[start + k * stride : start + k * stride + 1, :] for k in range(n)]
        return jnp.concatenate(rows + [jnp.zeros((8 - n, LANES), jnp.float32)], axis=0)

    size = halo_ref.shape[0]
    group = grp_ref[0]
    neighbours = (
        (lax.rem(group + size - 1, size), group > 0),
        (lax.rem(group + 1, size), group < size - 1),
    )
    for side, (source, inside) in enumerate(neighbours):
        halo = halo_ref.at[source]
        keep = jnp.where(inside, 1.0, 0.0)
        south = side == 0
        tiles = tile_ref.at[side].reshape(HALF * ROWBLOCK, LANES)
        rows_out = fixed.at[side].reshape(2 * HALF * 8, LANES)
        own = lambda p: p - HALO if south else 7 - (p - HALO)
        sent = lambda p: p if south else HALO - 1 - p
        base = 0 if south else (ROWS // 8 - 1) * ROWBLOCK
        m = [None]
        for p in range(1, total):
            row = []
            for j in range(TILES):
                if p < HALO:
                    at = HALF * SLOT + j * HALO + sent(p)
                    row.append(halo[at : at + 1, :])
                else:
                    at = base + j * 8 + own(p)
                    row.append(flat_mask[at : at + 1, :].astype(jnp.float32))
            m.append(row)
        for g, n in ((0, 8), (8, 8), (16, 2)):
            a = courant_ref[0] * table_ref[2 * side, g : g + 8, :]
            b = courant_ref[0] * table_ref[2 * side + 1, g : g + 8, :]
            c = 1.0 - a - b
            e = []
            for p in range(total):
                if p < HALO:
                    e.append([keep * eight(halo, g * SLOT + j * HALO + sent(p), n, SLOT) for j in range(TILES)])
                else:
                    e.append([eight(tiles, g * ROWBLOCK + j * 8 + own(p), n, ROWBLOCK) for j in range(TILES)])
            for k in range(SUBSTEPS):
                new = [None] * total
                for p in range(k + 1, total):
                    first = shifted(e[p], south) if g < 16 else None
                    second = shifted(e[p], not south) if g > 0 else None
                    if g == 0:
                        x = first
                    elif g == 16:
                        x = second
                    else:
                        x = [jnp.where(sub == 0, f, s) for f, s in zip(first, second)]
                    new[p] = [m[p][j] * (c * e[p][j] + a * x[j] + b * e[p - 1][j]) for j in range(TILES)]
                e = new
            for p in range(HALO, total):
                y = p - HALO if south else EDGE - 1 - (p - HALO)
                for j in range(TILES):
                    at = ((y // 2) * HALF + g) * 8 + 2 * j + y % 2
                    if n == 8:
                        rows_out[pl.ds(at, n, stride=8), :] = e[p][j]
                    else:
                        for k in range(n):
                            rows_out[at + 8 * k : at + 8 * k + 1, :] = e[p][j][k : k + 1]
        for i in range(2):
            place = PLACE[i if south else 30 + i]
            put = pltpu.make_async_copy(
                fixed.at[side, i], p_ref.at[place, pl.ds(side * HALF, HALF)], sem.at[2 * side + i]
            )
            put.start()
            puts.append(put)
    for put in puts:
        put.wait()


def edges(group, tiles, courant, mask, halos, inner):
    table = np.zeros((4, 24, LANES), np.float32)
    for side in range(2):
        ds = slice(side * HALF, (side + 1) * HALF)
        table[2 * side, :HALF] = np.abs(COS[ds])[:, None]
        table[2 * side + 1, :HALF] = np.abs(SIN[ds])[:, None]
    vmem = pl.BlockSpec(memory_space=pltpu.VMEM)
    hbm = pl.BlockSpec(memory_space=pl.ANY)
    return pl.pallas_call(
        edges_kernel,
        in_specs=[pl.BlockSpec(memory_space=pltpu.SMEM)] * 2 + [vmem, vmem, vmem, vmem, hbm],
        out_specs=hbm,
        out_shape=pltpu.HBM(inner.shape, inner.dtype),
        scratch_shapes=[pltpu.VMEM((2, 2, HALF, 8, LANES), jnp.float32), pltpu.SemaphoreType.DMA((4,))],
        input_output_aliases={6: 0},
        compiler_params=pltpu.CompilerParams(vmem_limit_bytes=4 * MIB),
        name="edges",
    )(group, courant, jnp.asarray(table), tiles, mask, halos, in_hbm(inner))


def pick_kernel(grp_ref, cells_ref, place_ref, source_ref, *refs):
    *out_refs, p_ref, sem = refs
    copy = pltpu.make_async_copy(source_ref, p_ref.at[pl.ds(0, 32 * NDIR * 8)], sem)
    copy.start()
    copy.wait()
    group = grp_ref[0]
    count = len(out_refs)
    lane = lax.broadcasted_iota(jnp.int32, (NDIR, LANES), 1)
    points = LANES // count
    for k, out in enumerate(out_refs):
        owner = lax.rem(group + k, count)
        nests = out.shape[0]

        def nest_body(n, carry):
            def point_body(p, acc):
                for u in range(8):
                    col = group * points + p * 8 + u
                    cell = lax.bitwise_and(cells_ref[owner * nests + n, col], ROWS * COLS - 1)
                    y = lax.shift_right_logical(cell, 9)
                    x = lax.bitwise_and(cell, COLS - 1)
                    row = place_ref[lax.shift_right_logical(y, 1)] * (NDIR * 8) + lax.shift_right_logical(x, 7) * 2 + lax.bitwise_and(y, 1)
                    got = p_ref[pl.ds(row, NDIR, stride=8), :]
                    turn = lax.bitwise_and(col - x, LANES - 1)
                    acc = jnp.where(lane == col, pltpu.roll(got, turn, 1), acc)
                return acc

            out[n] = lax.fori_loop(0, points // 8, point_body, jnp.zeros((NDIR, LANES), jnp.float32))
            return carry

        lax.fori_loop(0, nests, nest_body, 0)


def pick(group, cells, moved, count):
    nests = cells.shape[0] // count
    return pl.pallas_call(
        pick_kernel,
        in_specs=[
            pl.BlockSpec(memory_space=pltpu.SMEM),
            pl.BlockSpec(memory_space=pltpu.SMEM),
            pl.BlockSpec(memory_space=pltpu.SMEM),
            pl.BlockSpec(memory_space=pl.ANY),
        ],
        out_specs=[pl.BlockSpec(memory_space=pltpu.VMEM)] * count,
        out_shape=[jax.ShapeDtypeStruct((nests, NDIR, LANES), jnp.float32)] * count,
        scratch_shapes=[pltpu.VMEM((32 * NDIR * 8 + 64, LANES), jnp.float32), pltpu.SemaphoreType.DMA],
        compiler_params=pltpu.CompilerParams(vmem_limit_bytes=8 * MIB),
        cost_estimate=pl.CostEstimate(flops=10_000_000, bytes_accessed=6_000_000, transcendentals=0),
        name="pick",
    )(group, cells, jnp.asarray(PLACE, jnp.int32), in_hbm(moved.reshape(32 * NDIR * 8, LANES)))


def merge_kernel(*refs):
    *ins, out = refs
    nests = ins[0].shape[0]
    for n in range(nests):
        total = ins[0][n]
        for r in ins[1:]:
            total = total + r[n]
        whole = NDIR // 8 * 8
        out[pl.ds(n, whole, stride=nests), :] = total[:whole]
        for d in range(whole, NDIR):
            out[d * nests + n : d * nests + n + 1, :] = total[d : d + 1]


def merge(parts):
    nests = parts[0].shape[0]
    out = pl.pallas_call(
        merge_kernel,
        out_shape=jax.ShapeDtypeStruct((NDIR * nests, LANES), jnp.float32),
        compiler_params=pltpu.CompilerParams(vmem_limit_bytes=4 * MIB),
        name="merge",
    )(*parts)
    return out.reshape(NDIR, nests, LANES)


FCHUNK = 4
NCHUNK = NFREQ // FCHUNK


def source_kernel(recv_ref, u_ref, v_ref, out_ref, buf, outbuf, sem, osem):
    put = lambda c: pltpu.make_async_copy(
        outbuf.at[pl.ds(c * FCHUNK, FCHUNK)], out_ref.at[pl.ds(c * FCHUNK, FCHUNK)], osem.at[c]
    )
    fetch = lambda c: pltpu.make_async_copy(recv_ref.at[pl.ds(c * FCHUNK, FCHUNK)], buf.at[pl.ds(c * FCHUNK, FCHUNK)], sem.at[c])
    for c in range(NCHUNK):
        fetch(c).start()
    total = jnp.zeros((8, LANES), jnp.float32)
    weighted = jnp.zeros((8, LANES), jnp.float32)
    for p, f in enumerate(ORDER):
        if p % FCHUNK == 0:
            fetch(p // FCHUNK).wait()
        s = jnp.sum(buf[p], axis=0)
        total = total + s
        weighted = weighted + s * float(SCALE[f] * SCALE[f])
    m0 = total * (1.0 / (NFREQ * NDIR))
    q = weighted * (1.0 / (NFREQ * NDIR))
    ratio = jnp.maximum(m0, 0.05) / jnp.maximum(q, 0.1)
    steep = m0 / 0.3
    base = ratio * (steep * steep)
    u = u_ref[...]
    v = v_ref[...]

    for c in range(NCHUNK):
        fs = range(c * FCHUNK, (c + 1) * FCHUNK)
        loss = [base * float(0.1 * SCALE[f] ** 3 * LOG2E) for f in fs]
        for d in range(NDIR):
            proj = u * float(COS[d]) + v * float(SIN[d])
            for i, f in enumerate(fs):
                gain = jnp.maximum(proj * float(0.05 * SCALE[f] ** 2 * LOG2E) - float(0.05 * SCALE[f] * LOG2E), 0.0)
                outbuf[f, d] = buf[PLACE[f], d] * jnp.exp2(gain - loss[i])
        put(c).start()
    for c in range(NCHUNK):
        put(c).wait()


def sources(recv, wind_u, wind_v):
    tile = lambda w: w.reshape(2, TILES, LANES).transpose(1, 0, 2).reshape(8, LANES)
    shape = (NFREQ, NDIR, 8, LANES)
    out = pl.pallas_call(
        source_kernel,
        in_specs=[pl.BlockSpec(memory_space=pl.ANY)] + [pl.BlockSpec(memory_space=pltpu.VMEM)] * 2,
        out_specs=pl.BlockSpec(memory_space=pltpu.HBM),
        out_shape=jax.ShapeDtypeStruct(shape, jnp.float32),
        scratch_shapes=[
            pltpu.VMEM(shape, jnp.float32),
            pltpu.VMEM(shape, jnp.float32),
            pltpu.SemaphoreType.DMA((NCHUNK,)),
            pltpu.SemaphoreType.DMA((NCHUNK,)),
        ],
        compiler_params=pltpu.CompilerParams(vmem_limit_bytes=12 * MIB),
        name="sources",
    )(in_hbm(recv), tile(wind_u), tile(wind_v))
    out = out.reshape(NFREQ, NDIR, TILES, 2, LANES).transpose(0, 1, 3, 2, 4)
    return out.reshape(NFREQ, NDIR, 1, 2, COLS)


def per_device(spectrum, courant, sea_mask, wind_u, wind_v, boundary_cells):
    size = lax.axis_size("grp")
    group = lax.axis_index("grp").astype(jnp.int32).reshape(1)
    block = tiled(spectrum.reshape(NDIR, ROWS, COLS))
    mask = tiled(sea_mask.reshape(ROWS, COLS))
    halos = pack(group, block, mask, size)
    halos = lax.all_to_all(halos, "grp", split_axis=0, concat_axis=0, tiled=True)
    inner, tiles = interior(block, courant, mask)
    result = edges(group, tiles, courant, mask, halos, inner)
    moved = lax.all_to_all(result, "comp", split_axis=0, concat_axis=0, axis_index_groups=[list(ORDER)], tiled=True)
    picked = pick(group, boundary_cells, result, size)
    parts = [picked[0]]
    for k in range(1, size):
        parts.append(lax.ppermute(picked[k], "grp", [(i, (i + k) % size) for i in range(size)]))
    boundary = merge(parts)[None]
    updated = sources(moved, wind_u.reshape(2, COLS), wind_v.reshape(2, COLS))
    return updated, boundary


def solution(mesh):
    placed = (
        P("comp", None, "grp", None, None),
        P("comp"),
        P("grp", None, None),
        P("grp", "comp", None),
        P("grp", "comp", None),
        P(),
    )
    return jax.shard_map(
        per_device,
        mesh=mesh,
        in_specs=placed,
        out_specs=(P(None, None, "grp", "comp", None), P("comp", None, "grp", None)),
        check_vma=False,
    )
```

```python
import functools

import jax
import jax.numpy as jnp
import numpy as np
from jax import lax
from jax.experimental import pallas as pl
from jax.experimental.pallas import tpu as pltpu
from jax.sharding import PartitionSpec as P

NDIR = 36
NFREQ = 32
SUBSTEPS = 3
HALF = NDIR // 2
QUART = NDIR // 4
ROWS = 64
COLS = 512
LANES = 128
TILES = COLS // LANES
HALO = 3
SLOTS = HALF + 2
SLOT = TILES * HALO
ROWBLOCK = TILES * 8
MIB = 1024 * 1024

THETA = (2.0 * np.pi * np.arange(NDIR) / NDIR).astype(np.float32)
COS = np.cos(THETA).astype(np.float32)
SIN = np.sin(THETA).astype(np.float32)
SCALE = (0.3 * np.float32(1.1) ** np.arange(NFREQ, dtype=np.float32)).astype(np.float32)
LOG2E = 1.4426950408889634

ORDER = (15, 27, 28, 26, 21, 18, 24, 3, 9, 25, 6, 13, 7, 31, 20, 12, 1, 17, 23, 2, 30, 14, 16, 10, 0, 22, 5, 4, 8, 11, 19, 29)
PLACE = tuple(int(p) for p in np.argsort(ORDER))


def tiled(value):
    lead = value.shape[:-2]
    n = len(lead)
    value = value.reshape(*lead, ROWS // 8, 8, TILES, LANES)
    return value.transpose(*range(n), n, n + 2, n + 1, n + 3)


def in_hbm(value):
    return pltpu.with_memory_space_constraint(value, pltpu.HBM)


def pack_kernel(grp_ref, spectrum_ref, mask_ref, out_ref, packed, mask_s, sem):
    size = out_ref.shape[0]
    group = grp_ref[0]
    sides = (
        (lax.rem(group + 1, size), 0, ROWS // 8 - 1, 8 - HALO),
        (lax.rem(group + size - 1, size), HALF, 0, 0),
    )
    rows, masks, puts = [], [], []
    for side, (slot, d, tile, low) in enumerate(sides):
        near = pl.ds(low, HALO)
        rows.append(
            pltpu.make_async_copy(
                spectrum_ref.at[pl.ds(d, HALF), tile, :, near], packed.at[side, pl.ds(0, HALF)], sem.at[side]
            )
        )
        masks.append(pltpu.make_async_copy(mask_ref.at[tile, :, near], mask_s.at[side], sem.at[2 + side]))
        puts.append(pltpu.make_async_copy(packed.at[side], out_ref.at[slot], sem.at[4 + side]))
    for copy in rows + masks:
        copy.start()
    for side in range(2):
        masks[side].wait()
        packed[side, HALF] = mask_s[side].astype(jnp.float32)
        packed[side, HALF + 1] = jnp.zeros((TILES, HALO, 1, LANES), jnp.float32)
    for side in range(2):
        rows[side].wait()
        puts[side].start()
    for copy in puts:
        copy.wait()


def pack(group, spectrum, mask, size):
    out = pl.pallas_call(
        pack_kernel,
        in_specs=[pl.BlockSpec(memory_space=pltpu.SMEM)] + [pl.BlockSpec(memory_space=pl.ANY)] * 2,
        out_specs=pl.BlockSpec(memory_space=pl.ANY),
        out_shape=pltpu.HBM((size, SLOTS, TILES, HALO, 1, LANES), jnp.float32),
        scratch_shapes=[
            pltpu.VMEM((2, SLOTS, TILES, HALO, 1, LANES), jnp.float32),
            pltpu.VMEM((2, TILES, HALO, 1, LANES), jnp.int32),
            pltpu.SemaphoreType.DMA((6,)),
        ],
        compiler_params=pltpu.CompilerParams(vmem_limit_bytes=2 * MIB),
        name="pack",
    )(group, in_hbm(spectrum[..., None, :]), in_hbm(mask[..., None, :]))
    return out.reshape(size, SLOTS * SLOT, LANES)


FETCH = 3
CHUNKS = NDIR // FETCH


def shifted(row, west):
    lane = lax.broadcasted_iota(jnp.int32, (8, LANES), 1)
    r = [pltpu.roll(v, 1 if west else LANES - 1, 1) for v in row]
    if west:
        return [jnp.where(lane == 0, r[j - 1], r[j]) for j in range(TILES)]
    return [jnp.where(lane == LANES - 1, r[(j + 1) % TILES], r[j]) for j in range(TILES)]


def interior_kernel(courant_ref, trig_ref, e_ref, mask_ref, out_ref, tile_ref, e_buf, out_buf, mask_s, sem, out_sem):
    fetch = lambda c: pltpu.make_async_copy(e_ref.at[pl.ds(c * FETCH, FETCH)], e_buf.at[pl.ds(c * FETCH, FETCH)], sem.at[c])
    put = lambda c: pltpu.make_async_copy(out_buf.at[:, pl.ds(c * FETCH, FETCH)], out_ref.at[:, pl.ds(c * FETCH, FETCH)], out_sem.at[c])
    for c in range(CHUNKS):
        fetch(c).start()
    sub = lax.broadcasted_iota(jnp.int32, (8, LANES), 0)
    mask_s[...] = mask_ref[...].astype(jnp.float32)

    def advance(south, west, first, i, carry):
        ds = [first + i * FETCH + u for u in range(FETCH)]
        many = range(FETCH)
        at, turn = (0, 1) if south else (7, 7)
        fetch(first // FETCH + i).wait()
        a = [courant_ref[0] * trig_ref[0, d] for d in ds]
        b = [courant_ref[0] * trig_ref[1, d] for d in ds]
        c = [1.0 - x - y for x, y in zip(a, b)]
        e = [[[e_buf[d, t, j] for j in range(TILES)] for t in range(8)] for d in ds]
        for u in many:
            for j in range(TILES):
                tile_ref[0 if south else 1, ds[u] - (0 if south else HALF), j] = e[u][at][j]
        for stage in range(SUBSTEPS):
            new = [[None] * 8 for _ in many]
            moved = [[[pltpu.roll(v, turn, 0) for v in row] for row in e[u]] for u in many]
            for u in many:
                for t in range(8):
                    x = shifted(e[u][t], west)
                    y = moved[u][t]
                    if t != at:
                        beyond = moved[u][t - 1 if south else t + 1]
                        y = [jnp.where(sub == at, beyond[j], y[j]) for j in range(TILES)]
                    new[u][t] = [mask_s[t, j] * (c[u] * e[u][t][j] + a[u] * x[j] + b[u] * y[j]) for j in range(TILES)]
            e = new
        odd, high = sub & 2 != 0, sub >= 4
        for u in many:
            for t in range(8):
                v = e[u][t]
                w = [
                    jnp.where(odd, pltpu.roll(v[1], 2, 0), v[0]),
                    jnp.where(odd, v[1], pltpu.roll(v[0], 6, 0)),
                    jnp.where(odd, pltpu.roll(v[3], 2, 0), v[2]),
                    jnp.where(odd, v[3], pltpu.roll(v[2], 6, 0)),
                ]
                out_buf[PLACE[4 * t], ds[u]] = jnp.where(high, pltpu.roll(w[2], 4, 0), w[0])
                out_buf[PLACE[4 * t + 1], ds[u]] = jnp.where(high, pltpu.roll(w[3], 4, 0), w[1])
                out_buf[PLACE[4 * t + 2], ds[u]] = jnp.where(high, w[2], pltpu.roll(w[0], 4, 0))
                out_buf[PLACE[4 * t + 3], ds[u]] = jnp.where(high, w[3], pltpu.roll(w[1], 4, 0))
        put(first // FETCH + i).start()
        return carry

    for q, (south, west) in enumerate(((True, True), (True, False), (False, False), (False, True))):
        lax.fori_loop(0, QUART // FETCH, functools.partial(advance, south, west, q * QUART), 0)
    for c in range(CHUNKS):
        put(c).wait()


def interior(spectrum, courant, mask):
    trig = np.stack([np.abs(COS), np.abs(SIN)])
    smem = pl.BlockSpec(memory_space=pltpu.SMEM)
    vmem = pl.BlockSpec(memory_space=pltpu.VMEM)
    hbm = pl.BlockSpec(memory_space=pl.ANY)
    return pl.pallas_call(
        interior_kernel,
        in_specs=[smem, smem, hbm, vmem],
        out_specs=[hbm, vmem],
        out_shape=[
            pltpu.HBM((32, NDIR, 8, LANES), jnp.float32),
            jax.ShapeDtypeStruct((2, HALF, TILES, 8, LANES), jnp.float32),
        ],
        scratch_shapes=[
            pltpu.VMEM((NDIR, ROWS // 8, TILES, 8, LANES), jnp.float32),
            pltpu.VMEM((32, NDIR, 8, LANES), jnp.float32),
            pltpu.VMEM((8, TILES, 8, LANES), jnp.float32),
            pltpu.SemaphoreType.DMA((CHUNKS,)),
            pltpu.SemaphoreType.DMA((CHUNKS,)),
        ],
        compiler_params=pltpu.CompilerParams(vmem_limit_bytes=12 * MIB),
        cost_estimate=pl.CostEstimate(flops=40_000_000, bytes_accessed=9_500_000, transcendentals=0),
        name="interior",
    )(courant, jnp.asarray(trig), in_hbm(spectrum), mask)


EDGE = 4


def edges_kernel(grp_ref, courant_ref, table_ref, tile_ref, mask_ref, halo_ref, p_in, p_ref, fixed, sem):
    del p_in
    sub = lax.broadcasted_iota(jnp.int32, (8, LANES), 0)
    flat_mask = mask_ref.reshape(ROWS * TILES, LANES)
    total = HALO + EDGE
    puts = []

    def eight(ref, start, n, stride):
        if n == 8:
            return ref[pl.ds(start, n, stride=stride), :]
        rows = [ref[start + k * stride : start + k * stride + 1, :] for k in range(n)]
        return jnp.concatenate(rows + [jnp.zeros((8 - n, LANES), jnp.float32)], axis=0)

    size = halo_ref.shape[0]
    group = grp_ref[0]
    neighbours = (
        (lax.rem(group + size - 1, size), group > 0),
        (lax.rem(group + 1, size), group < size - 1),
    )
    for side, (source, inside) in enumerate(neighbours):
        halo = halo_ref.at[source]
        keep = jnp.where(inside, 1.0, 0.0)
        south = side == 0
        tiles = tile_ref.at[side].reshape(HALF * ROWBLOCK, LANES)
        rows_out = fixed.at[side].reshape(2 * HALF * 8, LANES)
        own = lambda p: p - HALO if south else 7 - (p - HALO)
        sent = lambda p: p if south else HALO - 1 - p
        base = 0 if south else (ROWS // 8 - 1) * ROWBLOCK
        m = [None]
        for p in range(1, total):
            row = []
            for j in range(TILES):
                if p < HALO:
                    at = HALF * SLOT + j * HALO + sent(p)
                    row.append(halo[at : at + 1, :])
                else:
                    at = base + j * 8 + own(p)
                    row.append(flat_mask[at : at + 1, :].astype(jnp.float32))
            m.append(row)
        for g, n in ((0, 8), (8, 8), (16, 2)):
            a = courant_ref[0] * table_ref[2 * side, g : g + 8, :]
            b = courant_ref[0] * table_ref[2 * side + 1, g : g + 8, :]
            c = 1.0 - a - b
            e = []
            for p in range(total):
                if p < HALO:
                    e.append([keep * eight(halo, g * SLOT + j * HALO + sent(p), n, SLOT) for j in range(TILES)])
                else:
                    e.append([eight(tiles, g * ROWBLOCK + j * 8 + own(p), n, ROWBLOCK) for j in range(TILES)])
            for k in range(SUBSTEPS):
                new = [None] * total
                for p in range(k + 1, total):
                    first = shifted(e[p], south) if g < 16 else None
                    second = shifted(e[p], not south) if g > 0 else None
                    if g == 0:
                        x = first
                    elif g == 16:
                        x = second
                    else:
                        x = [jnp.where(sub == 0, f, s) for f, s in zip(first, second)]
                    new[p] = [m[p][j] * (c * e[p][j] + a * x[j] + b * e[p - 1][j]) for j in range(TILES)]
                e = new
            for p in range(HALO, total):
                y = p - HALO if south else EDGE - 1 - (p - HALO)
                for j in range(TILES):
                    at = ((y // 2) * HALF + g) * 8 + 2 * j + y % 2
                    if n == 8:
                        rows_out[pl.ds(at, n, stride=8), :] = e[p][j]
                    else:
                        for k in range(n):
                            rows_out[at + 8 * k : at + 8 * k + 1, :] = e[p][j][k : k + 1]
        for i in range(2):
            place = PLACE[i if south else 30 + i]
            put = pltpu.make_async_copy(
                fixed.at[side, i], p_ref.at[place, pl.ds(side * HALF, HALF)], sem.at[2 * side + i]
            )
            put.start()
            puts.append(put)
    for put in puts:
        put.wait()


def edges(group, tiles, courant, mask, halos, inner):
    table = np.zeros((4, 24, LANES), np.float32)
    for side in range(2):
        ds = slice(side * HALF, (side + 1) * HALF)
        table[2 * side, :HALF] = np.abs(COS[ds])[:, None]
        table[2 * side + 1, :HALF] = np.abs(SIN[ds])[:, None]
    vmem = pl.BlockSpec(memory_space=pltpu.VMEM)
    hbm = pl.BlockSpec(memory_space=pl.ANY)
    return pl.pallas_call(
        edges_kernel,
        in_specs=[pl.BlockSpec(memory_space=pltpu.SMEM)] * 2 + [vmem, vmem, vmem, vmem, hbm],
        out_specs=hbm,
        out_shape=pltpu.HBM(inner.shape, inner.dtype),
        scratch_shapes=[pltpu.VMEM((2, 2, HALF, 8, LANES), jnp.float32), pltpu.SemaphoreType.DMA((4,))],
        input_output_aliases={6: 0},
        compiler_params=pltpu.CompilerParams(vmem_limit_bytes=4 * MIB),
        name="edges",
    )(group, courant, jnp.asarray(table), tiles, mask, halos, in_hbm(inner))


def pick_kernel(grp_ref, cells_ref, place_ref, source_ref, *refs):
    *out_refs, p_ref, sem = refs
    copy = pltpu.make_async_copy(source_ref, p_ref.at[pl.ds(0, 32 * NDIR * 8)], sem)
    copy.start()
    copy.wait()
    group = grp_ref[0]
    count = len(out_refs)
    lane = lax.broadcasted_iota(jnp.int32, (NDIR, LANES), 1)
    points = LANES // count
    for k, out in enumerate(out_refs):
        owner = lax.rem(group + k, count)
        nests = out.shape[0]

        def nest_body(n, carry):
            def point_body(p, acc):
                for u in range(8):
                    col = group * points + p * 8 + u
                    cell = lax.bitwise_and(cells_ref[owner * nests + n, col], ROWS * COLS - 1)
                    y = lax.shift_right_logical(cell, 9)
                    x = lax.bitwise_and(cell, COLS - 1)
                    row = place_ref[lax.shift_right_logical(y, 1)] * (NDIR * 8) + lax.shift_right_logical(x, 7) * 2 + lax.bitwise_and(y, 1)
                    got = p_ref[pl.ds(row, NDIR, stride=8), :]
                    turn = lax.bitwise_and(col - x, LANES - 1)
                    acc = jnp.where(lane == col, pltpu.roll(got, turn, 1), acc)
                return acc

            out[n] = lax.fori_loop(0, points // 8, point_body, jnp.zeros((NDIR, LANES), jnp.float32))
            return carry

        lax.fori_loop(0, nests, nest_body, 0)


def pick(group, cells, moved, count):
    nests = cells.shape[0] // count
    return pl.pallas_call(
        pick_kernel,
        in_specs=[
            pl.BlockSpec(memory_space=pltpu.SMEM),
            pl.BlockSpec(memory_space=pltpu.SMEM),
            pl.BlockSpec(memory_space=pltpu.SMEM),
            pl.BlockSpec(memory_space=pl.ANY),
        ],
        out_specs=[pl.BlockSpec(memory_space=pltpu.VMEM)] * count,
        out_shape=[jax.ShapeDtypeStruct((nests, NDIR, LANES), jnp.float32)] * count,
        scratch_shapes=[pltpu.VMEM((32 * NDIR * 8 + 64, LANES), jnp.float32), pltpu.SemaphoreType.DMA],
        compiler_params=pltpu.CompilerParams(vmem_limit_bytes=8 * MIB),
        cost_estimate=pl.CostEstimate(flops=10_000_000, bytes_accessed=6_000_000, transcendentals=0),
        name="pick",
    )(group, cells, jnp.asarray(PLACE, jnp.int32), in_hbm(moved.reshape(32 * NDIR * 8, LANES)))


def merge_kernel(*refs):
    *ins, out = refs
    nests = ins[0].shape[0]
    for n in range(nests):
        total = ins[0][n]
        for r in ins[1:]:
            total = total + r[n]
        whole = NDIR // 8 * 8
        out[pl.ds(n, whole, stride=nests), :] = total[:whole]
        for d in range(whole, NDIR):
            out[d * nests + n : d * nests + n + 1, :] = total[d : d + 1]


def merge(parts):
    nests = parts[0].shape[0]
    out = pl.pallas_call(
        merge_kernel,
        out_shape=jax.ShapeDtypeStruct((NDIR * nests, LANES), jnp.float32),
        compiler_params=pltpu.CompilerParams(vmem_limit_bytes=4 * MIB),
        name="merge",
    )(*parts)
    return out.reshape(NDIR, nests, LANES)


FCHUNK = 4
NCHUNK = NFREQ // FCHUNK


def source_kernel(recv_ref, u_ref, v_ref, out_ref, buf, outbuf, sem, osem):
    put = lambda c: pltpu.make_async_copy(
        outbuf.at[pl.ds(c * FCHUNK, FCHUNK)], out_ref.at[pl.ds(c * FCHUNK, FCHUNK)], osem.at[c]
    )
    fetch = lambda c: pltpu.make_async_copy(recv_ref.at[pl.ds(c * FCHUNK, FCHUNK)], buf.at[pl.ds(c * FCHUNK, FCHUNK)], sem.at[c])
    for c in range(NCHUNK):
        fetch(c).start()
    total = jnp.zeros((8, LANES), jnp.float32)
    weighted = jnp.zeros((8, LANES), jnp.float32)
    for p, f in enumerate(ORDER):
        if p % FCHUNK == 0:
            fetch(p // FCHUNK).wait()
        s = jnp.sum(buf[p], axis=0)
        total = total + s
        weighted = weighted + s * float(SCALE[f] * SCALE[f])
    m0 = total * (1.0 / (NFREQ * NDIR))
    q = weighted * (1.0 / (NFREQ * NDIR))
    ratio = jnp.maximum(m0, 0.05) / jnp.maximum(q, 0.1)
    steep = m0 / 0.3
    base = ratio * (steep * steep)
    u = u_ref[...]
    v = v_ref[...]

    for c in range(NCHUNK):
        fs = range(c * FCHUNK, (c + 1) * FCHUNK)
        loss = [base * float(0.1 * SCALE[f] ** 3 * LOG2E) for f in fs]
        for d in range(NDIR):
            proj = u * float(COS[d]) + v * float(SIN[d])
            for i, f in enumerate(fs):
                gain = jnp.maximum(proj * float(0.05 * SCALE[f] ** 2 * LOG2E) - float(0.05 * SCALE[f] * LOG2E), 0.0)
                outbuf[f, d] = buf[PLACE[f], d] * jnp.exp2(gain - loss[i])
        put(c).start()
    for c in range(NCHUNK):
        put(c).wait()


def sources(recv, wind_u, wind_v):
    tile = lambda w: w.reshape(2, TILES, LANES).transpose(1, 0, 2).reshape(8, LANES)
    shape = (NFREQ, NDIR, 8, LANES)
    out = pl.pallas_call(
        source_kernel,
        in_specs=[pl.BlockSpec(memory_space=pl.ANY)] + [pl.BlockSpec(memory_space=pltpu.VMEM)] * 2,
        out_specs=pl.BlockSpec(memory_space=pltpu.HBM),
        out_shape=jax.ShapeDtypeStruct(shape, jnp.float32),
        scratch_shapes=[
            pltpu.VMEM(shape, jnp.float32),
            pltpu.VMEM(shape, jnp.float32),
            pltpu.SemaphoreType.DMA((NCHUNK,)),
            pltpu.SemaphoreType.DMA((NCHUNK,)),
        ],
        compiler_params=pltpu.CompilerParams(vmem_limit_bytes=12 * MIB),
        name="sources",
    )(in_hbm(recv), tile(wind_u), tile(wind_v))
    out = out.reshape(NFREQ, NDIR, TILES, 2, LANES).transpose(0, 1, 3, 2, 4)
    return out.reshape(NFREQ, NDIR, 1, 2, COLS)


def per_device(spectrum, courant, sea_mask, wind_u, wind_v, boundary_cells):
    size = lax.axis_size("grp")
    group = lax.axis_index("grp").astype(jnp.int32).reshape(1)
    block = tiled(spectrum.reshape(NDIR, ROWS, COLS))
    mask = tiled(sea_mask.reshape(ROWS, COLS))
    halos = pack(group, block, mask, size)
    halos = lax.all_to_all(halos, "grp", split_axis=0, concat_axis=0, tiled=True)
    inner, tiles = interior(block, courant, mask)
    result = edges(group, tiles, courant, mask, halos, inner)
    moved = lax.all_to_all(result, "comp", split_axis=0, concat_axis=0, axis_index_groups=[list(ORDER)], tiled=True)
    picked = pick(group, boundary_cells, result, size)
    parts = [picked[0]]
    for k in range(1, size):
        parts.append(lax.ppermute(picked[k], "grp", [(i, (i + k) % size) for i in range(size)]))
    boundary = merge(parts)[None]
    updated = sources(moved, wind_u.reshape(2, COLS), wind_v.reshape(2, COLS))
    return updated, boundary


def solution(mesh):
    placed = (
        P("comp", None, "grp", None, None),
        P("comp"),
        P("grp", None, None),
        P("grp", "comp", None),
        P("grp", "comp", None),
        P(),
    )
    return jax.shard_map(
        per_device,
        mesh=mesh,
        in_specs=placed,
        out_specs=(P(None, None, "grp", "comp", None), P("comp", None, "grp", None)),
        check_vma=False,
    )
```
